256 devices in a mesh: gx: 8 (over z), gy: 8 (over y_hi, x), gz: 4 (over y_lo, core).
Axes of the slice: x: 4, y: 4 (y_hi: 2, y_lo: 2; y = y_hi * 2 + y_lo), z: 8, core: 2. Of those that a mesh axis runs over, the one named last changes fastest.
Arguments:
- incumbent_wavenumber_normals: float32 [2, 256, 512, 512], P(None, ('gy', 'gz'), 'gx'), may hold values from -6 to 6
- renewed_wavenumber_normals: float32 [2, 256, 512, 512], P(None, ('gy', 'gz'), 'gx'), may hold values from -6 to 6
- jump_scale_factor: float32 [1], replicated, may hold values from 0.2 to 0.6
- unsintered_solidity: float32 [256, 512, 512], P('gx', 'gy', 'gz'), may hold values from 0.45 to 0.8
- opening_warmth_map: float32 [256, 512, 512], P('gx', 'gy', 'gz'), may hold values from 0.7 to 1.3
- detector_lattice_place: int32 [4096, 3], replicated, may hold values from 0 to 511, as said below
- recorded_detector_kelvin: float32 [4096], replicated, may hold values from 0.8 to 1.4
- incumbent_mismatch_cost: float32 [1], replicated, may hold values from 1 to 3
Outputs:
- suggested_arrhenius_threshold: float32 [256, 512, 512], P('gx', 'gy', 'gz')
- density: float32 [256, 512, 512], P('gx', 'gy', 'gz')
- ending_kelvin_array: float32 [256, 512, 512], P('gx', 'gy', 'gz')
- modelled_detector_kelvin: float32 [4096], replicated
- natural_admit_odds: float32 [1], replicated
The draws below stay inside these ranges and needn't reach their ends.
Inputs may be any that keep to these rules, and one draw needn't show every extreme that they name: `detector_lattice_place`: each row holds one sensor's cell as (x, y, z) with x below 256, y below 512 and z below 512; sensors may share a cell.
All inputs are finite; a program needn't handle non-finite values.
Results may differ from the reference program's by a relative error of at most 0.000094.
Values sent between devices are 32-bit elements; how exact they have to be, the bound alone decides.
A program may use at most 128 MiB of HBM per device.

```python
import jax
import jax.numpy as jnp
from jax import lax

MESH_EXTENT_EAST = 256
MESH_EXTENT_NORTH = 512
MESH_EXTENT_UPWARD = 512
STEPS = 3
S = 4096


def draw_detector_lattice_place(key, part):
    cell_x = jax.random.randint(jax.random.fold_in(key, 11), (S,), 0, MESH_EXTENT_EAST)
    cell_y = jax.random.randint(jax.random.fold_in(key, 12), (S,), 0, MESH_EXTENT_NORTH)
    cell_z = jax.random.randint(jax.random.fold_in(key, 13), (S,), 0, MESH_EXTENT_UPWARD)
    cell_x = cell_x.at[0].set(0)
    cell_y = cell_y.at[0].set(MESH_EXTENT_NORTH - 1)
    cell_z = cell_z.at[0].set(MESH_EXTENT_UPWARD - 1)
    return jnp.stack([cell_x, cell_y, cell_z], axis=1).astype(jnp.int32)


def levels(stream_key, extent, cuts, least, largest):
    def one(position, shards_of):
        heights = jax.random.uniform(jax.random.fold_in(jax.random.fold_in(stream_key, 6), position), (shards_of,), jnp.float32, least / len(cuts), largest / len(cuts))
        return jnp.repeat(jnp.exp(heights), extent[position] // shards_of).reshape((-1,) + (1,) * (len(extent) - position - 1))

    factor_of = one(*cuts[0])
    for cut in cuts[1:]:
        factor_of = factor_of * one(*cut)
    return factor_of


def bell_draw(key, dims, width, reach, split=(), held_as=jnp.bfloat16):
    gain = levels(key, dims, split, -0.22, 0.18) if split else 1.0
    drawn = jax.random.normal(key, dims, jnp.float32) * width * gain
    return jnp.minimum(jnp.maximum(drawn, -reach), reach).astype(held_as)


def setup_inputs(seed: int = 0) -> dict:
    seeds = jax.random.split(jax.random.key(seed), 9)
    incumbent_wavenumber_normals = bell_draw(seeds[0], (2, MESH_EXTENT_EAST, MESH_EXTENT_NORTH, MESH_EXTENT_UPWARD), 1.0, 6.0, ((1, 32), (2, 8)), jnp.float32)
    renewed_wavenumber_normals = bell_draw(seeds[1], (2, MESH_EXTENT_EAST, MESH_EXTENT_NORTH, MESH_EXTENT_UPWARD), 1.0, 6.0, ((1, 32), (2, 8)), jnp.float32)
    jump_scale_factor = jnp.clip(jax.random.uniform(seeds[2], (1,), jnp.float32, 0.2, 0.6), 0.2, 0.6)
    unsintered_solidity = jnp.clip(0.45 + 0.35000002 * jax.random.uniform(seeds[3], (MESH_EXTENT_EAST, MESH_EXTENT_NORTH, MESH_EXTENT_UPWARD), jnp.float32) ** levels(seeds[3], (MESH_EXTENT_EAST, MESH_EXTENT_NORTH, MESH_EXTENT_UPWARD), ((0, 8), (1, 8), (2, 4)), -0.2, 0.2), 0.45, 0.8)
    opening_warmth_map = jnp.clip(0.7 + 0.59999996 * jax.random.uniform(seeds[4], (MESH_EXTENT_EAST, MESH_EXTENT_NORTH, MESH_EXTENT_UPWARD), jnp.float32) ** levels(seeds[4], (MESH_EXTENT_EAST, MESH_EXTENT_NORTH, MESH_EXTENT_UPWARD), ((0, 8), (1, 8), (2, 4)), -0.2, 0.2), 0.7, 1.3)
    detector_lattice_place = draw_detector_lattice_place(jax.random.fold_in(seeds[8], 71), 0)
    recorded_detector_kelvin = jnp.clip(jax.random.uniform(seeds[6], (S,), jnp.float32, 0.8, 1.4), 0.8, 1.4)
    incumbent_mismatch_cost = jnp.clip(jax.random.uniform(seeds[7], (1,), jnp.float32, 1.0, 3.0), 1.0, 3.0)
    return {"incumbent_wavenumber_normals": incumbent_wavenumber_normals, "renewed_wavenumber_normals": renewed_wavenumber_normals, "jump_scale_factor": jump_scale_factor, "unsintered_solidity": unsintered_solidity, "opening_warmth_map": opening_warmth_map, "detector_lattice_place": detector_lattice_place, "recorded_detector_kelvin": recorded_detector_kelvin, "incumbent_mismatch_cost": incumbent_mismatch_cost}


def spectrum(length):
    wave = jnp.arange(length, dtype=jnp.int32)
    signed = jnp.where(wave < length // 2, wave, wave - length).astype(jnp.float32)
    shape = 1.0 / jnp.sqrt(1.0 + (signed / 8.0) ** 2)
    return shape / jnp.sqrt(jnp.sum(shape * shape))

def neighbours(padded):
    return [padded[2:, 1:-1, 1:-1], padded[:-2, 1:-1, 1:-1], padded[1:-1, 2:, 1:-1], padded[1:-1, :-2, 1:-1], padded[1:-1, 1:-1, 2:], padded[1:-1, 1:-1, :-2]]

def march_forward(heat_pad, solidity_margined, barrier_inner):
    warmth_map_components = heat_pad[1:-1, 1:-1, 1:-1]
    fractional_packing = solidity_margined[1:-1, 1:-1, 1:-1]
    conduct_pad = solidity_margined * solidity_margined
    conduct = conduct_pad[1:-1, 1:-1, 1:-1]
    conductive_stream = jnp.zeros_like(warmth_map_components)
    for heat_side, cond_side in zip(neighbours(heat_pad), neighbours(conduct_pad)):
        conductive_stream = conductive_stream + 0.5 * (conduct + cond_side) * (heat_side - warmth_map_components)
    densify_rate = jnp.exp(-barrier_inner / (warmth_map_components + 1.25)) * (1.0 - fractional_packing)
    return (warmth_map_components + 0.16 * (conductive_stream + 3.0 * densify_rate), fractional_packing + 0.64 * densify_rate)

def reference(incumbent_wavenumber_normals, renewed_wavenumber_normals, jump_scale_factor, unsintered_solidity, opening_warmth_map, detector_lattice_place, recorded_detector_kelvin, incumbent_mismatch_cost):
    beta = jump_scale_factor[0]
    mixed = jnp.sqrt(1.0 - beta * beta) * incumbent_wavenumber_normals + beta * renewed_wavenumber_normals
    amplitude = spectrum(MESH_EXTENT_EAST)[:, None, None] * spectrum(MESH_EXTENT_NORTH)[None, :, None] * spectrum(MESH_EXTENT_UPWARD)[None, None, :]
    spectral = lax.complex(mixed[0] * amplitude, mixed[1] * amplitude)
    field = jnp.real(jnp.fft.ifftn(spectral)) * (MESH_EXTENT_EAST * MESH_EXTENT_NORTH * MESH_EXTENT_UPWARD)
    suggested_arrhenius_threshold = 2.0 + 0.6 * jnp.tanh(field)
    warmth_map_components = opening_warmth_map - 1.25
    fractional_packing = unsintered_solidity
    for step in range(STEPS):
        warmth_map_components, fractional_packing = march_forward(jnp.pad(warmth_map_components, 1), jnp.pad(fractional_packing, 1), suggested_arrhenius_threshold)
    ending_kelvin_array = warmth_map_components + 1.25
    modelled_detector_kelvin = ending_kelvin_array[detector_lattice_place[:, 0], detector_lattice_place[:, 1], detector_lattice_place[:, 2]]
    residual_sumsq = 0.5 * jnp.mean(((modelled_detector_kelvin - recorded_detector_kelvin) / 0.2) ** 2)
    natural_admit_odds = incumbent_mismatch_cost - residual_sumsq
    return (suggested_arrhenius_threshold, fractional_packing, ending_kelvin_array, modelled_detector_kelvin, natural_admit_odds)
```

```python
import functools
import math

import jax
import jax.numpy as jnp
import ml_dtypes
import numpy as np
from jax import lax
from jax.experimental import pallas as pl
from jax.experimental.pallas import tpu as pltpu
from jax.sharding import PartitionSpec as P

MESH_EXTENT_EAST = 256
MESH_EXTENT_NORTH = 512
MESH_EXTENT_UPWARD = 512
STEPS = 3
S = 4096
CHUNKS = 4
MESH = pl.DeviceIdType.MESH
F32 = jnp.float32
BF16 = jnp.bfloat16
NT = (((1,), (1,)), ((), ()))


def spectrum(length):
    wave = np.arange(length)
    signed = np.where(wave < length // 2, wave, wave - length).astype(np.float64)
    shape = 1.0 / np.sqrt(1.0 + (signed / 8.0) ** 2)
    return shape / np.sqrt(np.sum(shape * shape))


def waves(places, numbers, length):
    angle = (places[:, None] * numbers[None, :] % length) * (2.0 * math.pi / length)
    scale = spectrum(length)[numbers][None, :]
    return np.cos(angle) * scale, np.sin(angle) * scale


def halves(table):
    high = table.astype(np.float32).astype(ml_dtypes.bfloat16)
    low = (table - high.astype(np.float64)).astype(np.float32).astype(ml_dtypes.bfloat16)
    return high, low


def tables(gx, gy, gz, nx, ny, nz):
    sub = nz // (gy * gz)
    part = sub // CHUNKS
    stacks = []
    for chunk in range(CHUNKS):
        places = np.concatenate(
            [
                z * (nz // gz) + y * sub + chunk * part + np.arange(part)
                for y in range(gy)
                for z in range(gz)
            ]
        )
        cosine, sine = waves(places, np.arange(nz), nz)
        stacks.append(np.concatenate(halves(np.concatenate([cosine, sine]))))
    depth = np.stack(stacks)
    cosine, sine = waves(np.arange(nx), np.arange(nx), nx)
    first = np.concatenate(halves(np.concatenate([cosine, sine])))
    width = ny // gx
    blocks = []
    for block in range(gx):
        cosine, sine = waves(np.arange(ny), block * width + np.arange(width), ny)
        blocks += [cosine.T, -sine.T]
    second = np.stack(halves(np.concatenate(blocks)))
    return depth, first, second


def split(values):
    high = values.astype(BF16)
    return high, (values - high.astype(F32)).astype(BF16)


def kernel(
    dims,
    beta,
    sensor_x,
    sensor_y,
    sensor_z,
    cost,
    inc,
    ren,
    w1_hbm,
    w2_hbm,
    w3_hbm,
    rho0,
    heat0,
    recorded,
    thr_out,
    rho_out,
    heat_out,
    model_out,
    odds_out,
    inc_v,
    ren_v,
    b_high,
    b_low,
    w1,
    w2,
    w3,
    send1,
    got1,
    send2,
    got2,
    send3,
    got3,
    thr,
    state,
    hx_send,
    hx_got,
    hy_send,
    hy_got,
    hz_send,
    hz_got,
    gathered,
    red_send,
    red_a,
    red_mid,
    red_b,
    red_fin,
    red_c,
    load_sem,
    out_sem,
    s1_sem,
    r1_sem,
    s2_sem,
    r2_sem,
    s3_sem,
    r3_sem,
    hs_sem,
    hr_sem,
    rs_sem,
    rr_sem,
):
    gx, gy, gz, nx, ny, nz = dims
    nd = gy * gz
    sub = nz // nd
    part = sub // CHUNKS
    bx, by, bz = nx // gx, ny // gy, nz // gz
    half = bx // 2
    kx_own = nx // nd
    ix, iy, iz = lax.axis_index("gx"), lax.axis_index("gy"), lax.axis_index("gz")
    me = iy * gz + iz

    def plane_device(k):
        other = lax.rem(me + k, nd)
        return other, (ix, other // gz, lax.rem(other, gz))

    def line_device(k):
        other = lax.rem(ix + k, gx)
        return other, (other, iy, iz)

    def row_device(k):
        other = lax.rem(iy + k, gy)
        return other, (ix, other, iz)

    loads = [
        pltpu.make_async_copy(inc, inc_v, load_sem.at[0]),
        pltpu.make_async_copy(ren, ren_v, load_sem.at[1]),
        pltpu.make_async_copy(w1_hbm, w1, load_sem.at[2]),
        pltpu.make_async_copy(heat0, state.at[0, 0, pl.ds(1, bx), pl.ds(8, by), :], load_sem.at[3]),
        pltpu.make_async_copy(rho0, state.at[0, 1, pl.ds(1, bx), pl.ds(8, by), :], load_sem.at[4]),
        pltpu.make_async_copy(w2_hbm, w2, load_sem.at[5]),
        pltpu.make_async_copy(w3_hbm, w3, load_sem.at[6]),
    ]
    for load in loads:
        load.start()

    barrier = pltpu.get_barrier_semaphore()

    def greet_plane(k, carry):
        pl.semaphore_signal(barrier, inc=1, device_id=plane_device(k)[1], device_id_type=MESH)
        return carry

    def greet_line(k, carry):
        pl.semaphore_signal(barrier, inc=1, device_id=line_device(k)[1], device_id_type=MESH)
        return carry

    lax.fori_loop(1, nd, greet_plane, 0)
    lax.fori_loop(1, gx, greet_line, 0)

    lane = lax.broadcasted_iota(jnp.int32, (1, 128), 1)
    sign = jnp.where(lane < 64, -1.0, 1.0).astype(F32)
    first_half = lane < 64

    sides = [("x", ix, gx, 0), ("y", iy, gy, 1), ("z", iz, gz, 2)]
    got = {"x": hx_got, "y": hy_got, "z": hz_got}
    sent = {"x": hx_send, "y": hy_send, "z": hz_send}
    outside = jnp.where(lane < bx, 1.25, 0.0).astype(F32)
    for name, place, count, number in sides:
        for end in range(2):
            edge = place == (0 if end == 0 else count - 1)

            @pl.when(edge)
            def _(name=name, end=end):
                for step in range(STEPS):
                    if name == "z":
                        hz_got[step, end] = jnp.broadcast_to(outside, hz_got.shape[2:])
                    else:
                        ref = got[name]
                        ref[step, end, 0] = jnp.full(ref.shape[3:], 1.25, F32)
                        ref[step, end, 1] = jnp.zeros(ref.shape[3:], F32)

    loads[0].wait()
    loads[1].wait()
    weight = jnp.full((1, 128), beta[0], F32)
    keep = jnp.sqrt(1.0 - weight * weight)[:, :1]
    fresh = weight[:, :1]

    def mix(k, carry):
        for part_of in range(2):
            mixed = keep * inc_v[part_of, k] + fresh * ren_v[part_of, k]
            high, low = split(mixed)
            rows = pl.ds(pl.multiple_of(k * 128 + part_of * 64, 64), 64)
            b_high[rows, :] = high
            b_low[rows, :] = low
        return carry

    lax.fori_loop(0, kx_own, mix, 0)
    loads[2].wait()
    pl.semaphore_wait(barrier, nd + gx - 2)

    rows1 = nd * part

    def stage1(c):
        flat = send1.at[c].reshape(rows1 * kx_own, 128)
        for q in range(kx_own // 2):
            right = pl.ds(q * 256, 256)
            top = lax.dot_general(w1[c], b_high[right, :], NT, preferred_element_type=F32)
            low = lax.dot_general(
                w1[c, pl.ds(0, 2 * rows1), :], b_low[right, :], NT, preferred_element_type=F32
            )
            total = top[: 2 * rows1] + top[2 * rows1 :] + low
            for side in range(2):
                cut = slice(side * 128, side * 128 + 128)
                cosines = total[:rows1, cut]
                sines = total[rows1:, cut]
                flat[pl.ds(2 * q + side, rows1, stride=kx_own), :] = cosines + sign * pltpu.roll(
                    sines, 64, 1
                )

        pltpu.make_async_copy(
            send1.at[c, pl.ds(me * part, part)],
            got1.at[c, :, pl.ds(pl.multiple_of(me * kx_own, kx_own), kx_own), :],
            r1_sem.at[c],
        ).start()

        def push(k, carry):
            other, device = plane_device(k)
            pltpu.make_async_remote_copy(
                src_ref=send1.at[c, pl.ds(other * part, part)],
                dst_ref=got1.at[c, :, pl.ds(pl.multiple_of(me * kx_own, kx_own), kx_own), :],
                send_sem=s1_sem.at[c],
                recv_sem=r1_sem.at[c],
                device_id=device,
                device_id_type=MESH,
            ).start()
            return carry

        lax.fori_loop(1, nd, push, 0)

    def stage2(c):
        pltpu.make_async_copy(got1.at[c], got1.at[c], r1_sem.at[c]).wait()

        def pair(p, carry):
            values = jnp.concatenate([got1[c, 2 * p], got1[c, 2 * p + 1]], axis=1)
            high, low = split(values)
            top = jnp.dot(w2[...], high, preferred_element_type=F32)
            bottom = jnp.dot(w2[pl.ds(0, 2 * nx), :], low, preferred_element_type=F32)
            total = top[: 2 * nx] + top[2 * nx :] + bottom
            for side in range(2):
                cut = slice(side * 128, side * 128 + 128)
                send2[c, 2 * p + side] = total[:nx, cut] + sign * pltpu.roll(total[nx:, cut], 64, 1)
            return carry

        lax.fori_loop(0, part // 2, pair, 0)
        pltpu.make_async_copy(
            send2.at[c, :, pl.ds(pl.multiple_of(ix * bx, bx), bx), :], got2.at[c, ix], r2_sem.at[c]
        ).start()

        def push(k, carry):
            other, device = line_device(k)
            pltpu.make_async_remote_copy(
                src_ref=send2.at[c, :, pl.ds(pl.multiple_of(other * bx, bx), bx), :],
                dst_ref=got2.at[c, ix],
                send_sem=s2_sem.at[c],
                recv_sem=r2_sem.at[c],
                device_id=device,
                device_id_type=MESH,
            ).start()
            return carry

        lax.fori_loop(1, gx, push, 0)

    def stage3(c):
        pltpu.make_async_copy(got2.at[c], got2.at[c], r2_sem.at[c]).wait()
        values = jnp.concatenate(
            [got2[c, g].reshape(part * bx, 128) for g in range(gx)], axis=1
        )
        high, low = split(values)
        rows = part * bx
        both = jnp.concatenate([high, low], axis=0)
        for t in range(ny // 256):
            columns = pl.ds(t * 256, 256)
            top = jnp.dot(both, w3[0, :, columns], preferred_element_type=F32)
            field = (
                top[:rows]
                + top[rows:]
                + jnp.dot(high, w3[1, :, columns], preferred_element_type=F32)
            )
            energy = 2.0 + 0.6 * jnp.tanh(field)
            for side in range(2):
                tile = energy[:, side * 128 : side * 128 + 128].reshape(part, 2, half, 128)
                near, far = tile[:, 0], tile[:, 1]
                near = near.reshape(part * half, 128)
                far = far.reshape(part * half, 128)
                j = 4 * t + 2 * side
                send3[c, j] = jnp.where(first_half, near, pltpu.roll(far, 64, 1))
                send3[c, j + 1] = jnp.where(first_half, pltpu.roll(near, 64, 1), far)
        target = got3.at[
            pl.ds(pl.multiple_of((iy * sub + c * part) * half, part * half), part * half), :
        ]
        pltpu.make_async_copy(send3.at[c, iy], target, r3_sem.at[0]).start()

        def push(k, carry):
            other, device = row_device(k)
            pltpu.make_async_remote_copy(
                src_ref=send3.at[c, other],
                dst_ref=target,
                send_sem=s3_sem.at[0],
                recv_sem=r3_sem.at[0],
                device_id=device,
                device_id_type=MESH,
            ).start()
            return carry

        lax.fori_loop(1, gy, push, 0)

    def exchange(step, now):
        def pack(x, carry):
            for f in range(2):
                plane = state[now, f, x + 1, pl.ds(8, by), :]
                hy_send[step, 0, f, pl.ds(x, 1), :] = plane[:1]
                hy_send[step, 1, f, pl.ds(x, 1), :] = plane[by - 1 :]
                here = lane == f * bx + x
                hz_send[step, 0] = jnp.where(
                    here, pltpu.roll(plane, f * bx + x, 1), hz_send[step, 0]
                )
                hz_send[step, 1] = jnp.where(
                    here, pltpu.roll(plane, f * bx + x + 1, 1), hz_send[step, 1]
                )
            return carry

        hz_send[step] = jnp.zeros(hz_send.shape[1:], F32)
        lax.fori_loop(0, bx, pack, 0)
        for f in range(2):
            hx_send[step, 0, f] = state[now, f, 1, pl.ds(8, by), :]
            hx_send[step, 1, f] = state[now, f, bx, pl.ds(8, by), :]
        for name, place, count, number in sides:
            for end in range(2):
                move = -1 if end == 0 else 1
                inner = place > 0 if end == 0 else place < count - 1
                device = [ix, iy, iz]
                device[number] = device[number] + move

                @pl.when(inner)
                def _(name=name, end=end, device=tuple(device), number=number):
                    pltpu.make_async_remote_copy(
                        src_ref=sent[name].at[step, end],
                        dst_ref=got[name].at[step, 1 - end],
                        send_sem=hs_sem.at[step, number, end],
                        recv_sem=hr_sem.at[step, number, 1 - end],
                        device_id=device,
                        device_id_type=MESH,
                    ).start()

    def receive(step, now):
        for name, place, count, number in sides:
            for end in range(2):
                inner = place > 0 if end == 0 else place < count - 1

                @pl.when(inner)
                def _(name=name, end=end, number=number):
                    ref = got[name].at[step, end]
                    pltpu.make_async_copy(ref, ref, hr_sem.at[step, number, end]).wait()

        for f in range(2):
            state[now, f, 0, pl.ds(8, by), :] = hx_got[step, 0, f]
            state[now, f, bx + 1, pl.ds(8, by), :] = hx_got[step, 1, f]

        def unpack(x, carry):
            for f in range(2):
                state[now, f, x + 1, pl.ds(7, 1), :] = hy_got[step, 0, f, pl.ds(x, 1), :]
                state[now, f, x + 1, pl.ds(8 + by, 1), :] = hy_got[step, 1, f, pl.ds(x, 1), :]
            return carry

        lax.fori_loop(0, bx, unpack, 0)

    def advance(step, now):
        def plane(x, carry):
            def at(f, dx, dy):
                return state[now, f, x + 1 + dx, pl.ds(8 + dy, by), :]

            heat, rho = at(0, 0, 0), at(1, 0, 0)
            cond = rho * rho
            flux = jnp.zeros_like(heat)
            around = [
                (at(0, 1, 0), at(1, 1, 0)),
                (at(0, -1, 0), at(1, -1, 0)),
                (at(0, 0, 1), at(1, 0, 1)),
                (at(0, 0, -1), at(1, 0, -1)),
            ]
            for end in range(2):
                packed = hz_got[step, end]
                edge = 0 if end == 0 else 127
                turn = 1 if end == 0 else 127
                pair = []
                for f, values in ((0, heat), (1, rho)):
                    shift = lax.rem(edge + 256 - f * bx - x, 128)
                    pair.append(
                        jnp.where(
                            lane == edge, pltpu.roll(packed, shift, 1), pltpu.roll(values, turn, 1)
                        )
                    )
                around.append(tuple(pair))
            for heat_side, rho_side in around:
                flux = flux + (cond + rho_side * rho_side) * (heat_side - heat)
            growth = jnp.exp(-thr[x] / heat) * (1.0 - rho)
            state[1 - now, 0, x + 1, pl.ds(8, by), :] = heat + 0.16 * (0.5 * flux + 3.0 * growth)
            state[1 - now, 1, x + 1, pl.ds(8, by), :] = rho + 0.64 * growth
            return carry

        lax.fori_loop(0, bx, plane, 0)

    def pipeline(i, carry):
        @pl.when(i < CHUNKS)
        def _():
            stage1(i)

        @pl.when(i == 0)
        def _():
            for load in loads[3:]:
                load.wait()
            exchange(0, 0)

        @pl.when((i >= 1) & (i <= CHUNKS))
        def _():
            stage2(i - 1)

        @pl.when(i >= 2)
        def _():
            stage3(i - 2)

        return carry

    lax.fori_loop(0, CHUNKS + 2, pipeline, 0)

    pltpu.make_async_copy(got3, got3, r3_sem.at[0]).wait()
    for x in range(half):
        turned = got3[pl.ds(x, bz, stride=half), :].T
        thr[x] = turned[:by]
        thr[half + x] = turned[by:]
    thr_copy = pltpu.make_async_copy(thr, thr_out, out_sem.at[0])
    thr_copy.start()

    for step in range(STEPS):
        now = step % 2
        if step:
            exchange(step, now)
        receive(step, now)
        advance(step, now)
    last = STEPS % 2
    heat_copy = pltpu.make_async_copy(
        state.at[last, 0, pl.ds(1, bx), pl.ds(8, by), :], heat_out, out_sem.at[1]
    )
    rho_copy = pltpu.make_async_copy(
        state.at[last, 1, pl.ds(1, bx), pl.ds(8, by), :], rho_out, out_sem.at[2]
    )
    heat_copy.start()
    rho_copy.start()

    def look(g, carry):
        rows = []
        for k in range(8):
            s = g * 8 + k
            row = state[last, 0, sensor_x[s], pl.ds(sensor_y[s], 1), :]
            rows.append(jnp.where(lane == sensor_z[s], row, 0.0))
        gathered[pl.ds(pl.multiple_of(g * 8, 8), 8), :] = jnp.concatenate(rows, axis=0)
        return carry

    lax.fori_loop(0, S // 8, look, 0)
    ones = jnp.ones((8, 128), F32)
    per = S // 128 // gx
    for block in range(gx):
        red_send[block] = jnp.zeros((8, 128), F32)
        for k in range(per):
            values = gathered[pl.ds((block * per + k) * 128, 128), :]
            sums = lax.dot_general(
                ones, values, NT, precision=lax.Precision.HIGHEST, preferred_element_type=F32
            )
            red_send[block, pl.ds(k, 1), :] = sums[:1]

    pltpu.make_async_copy(red_send.at[ix], red_a.at[ix], rr_sem.at[0]).start()

    def push_a(k, carry):
        other, device = line_device(k)
        pltpu.make_async_remote_copy(
            src_ref=red_send.at[other],
            dst_ref=red_a.at[ix],
            send_sem=rs_sem.at[0],
            recv_sem=rr_sem.at[0],
            device_id=device,
            device_id_type=MESH,
        ).start()
        return carry

    lax.fori_loop(1, gx, push_a, 0)
    pltpu.make_async_copy(red_a, red_a, rr_sem.at[0]).wait()
    red_mid[...] = jnp.sum(red_a[...], axis=0)
    pltpu.make_async_copy(red_mid, red_b.at[me], rr_sem.at[1]).start()

    def push_b(k, carry):
        other, device = plane_device(k)
        pltpu.make_async_remote_copy(
            src_ref=red_mid,
            dst_ref=red_b.at[me],
            send_sem=rs_sem.at[1],
            recv_sem=rr_sem.at[1],
            device_id=device,
            device_id_type=MESH,
        ).start()
        return carry

    lax.fori_loop(1, nd, push_b, 0)
    pltpu.make_async_copy(red_b, red_b, rr_sem.at[1]).wait()
    red_fin[...] = jnp.sum(red_b[...], axis=0)
    pltpu.make_async_copy(red_fin, red_c.at[ix], rr_sem.at[2]).start()

    def push_c(k, carry):
        other, device = line_device(k)
        pltpu.make_async_remote_copy(
            src_ref=red_fin,
            dst_ref=red_c.at[ix],
            send_sem=rs_sem.at[2],
            recv_sem=rr_sem.at[2],
            device_id=device,
            device_id_type=MESH,
        ).start()
        return carry

    lax.fori_loop(1, gx, push_c, 0)
    pltpu.make_async_copy(red_c, red_c, rr_sem.at[2]).wait()
    misfit = jnp.zeros((per, 128), F32)
    for block in range(gx):
        values = red_c[block, pl.ds(0, per), :]
        model_out[pl.ds(block * per, per), :] = values
        gap = (values - recorded[pl.ds(block * per, per), :]) / 0.2
        misfit = misfit + gap * gap
    odds_out[0] = cost[0] - 0.5 * (jnp.sum(misfit) / S)

    def drain(ref, sem):
        pltpu.make_async_copy(ref, ref, sem).wait()

    def drain_chunk(c, carry):
        drain(send1.at[c, pl.ds(0, (nd - 1) * part)], s1_sem.at[c])
        drain(send2.at[c, :, pl.ds(0, nx - bx), :], s2_sem.at[c])
        return carry

    lax.fori_loop(0, CHUNKS, drain_chunk, 0)
    drain(send3.at[:, pl.ds(0, gy - 1)], s3_sem.at[0])
    for name, place, count, number in sides:
        for end in range(2):
            inner = place > 0 if end == 0 else place < count - 1

            @pl.when(inner)
            def _(name=name, end=end, number=number):
                for step in range(STEPS):
                    drain(sent[name].at[step, end], hs_sem.at[step, number, end])

    drain(red_a.at[pl.ds(0, gx - 1)], rs_sem.at[0])
    drain(red_b.at[pl.ds(0, nd - 1)], rs_sem.at[1])
    drain(red_c.at[pl.ds(0, gx - 1)], rs_sem.at[2])
    thr_copy.wait()
    heat_copy.wait()
    rho_copy.wait()


def solution(mesh):
    gx, gy, gz = (mesh.shape[name] for name in ("gx", "gy", "gz"))
    nx, ny, nz = MESH_EXTENT_EAST, MESH_EXTENT_NORTH, MESH_EXTENT_UPWARD
    depth, first, second = tables(gx, gy, gz, nx, ny, nz)
    nd = gy * gz
    sub = nz // nd
    part = sub // CHUNKS
    bx, by, bz = nx // gx, ny // gy, nz // gz
    kx_own, ky_own = nx // nd, ny // gx

    def body(incumbent, renewed, beta, rho, heat, place, recorded, cost):
        local_x = place[:, 0] - lax.axis_index("gx") * bx
        local_y = place[:, 1] - lax.axis_index("gy") * by
        local_z = place[:, 2] - lax.axis_index("gz") * bz
        own = (
            (local_x >= 0)
            & (local_x < bx)
            & (local_y >= 0)
            & (local_y < by)
            & (local_z >= 0)
            & (local_z < bz)
        )
        sensor_x = jnp.clip(local_x, 0, bx - 1) + 1
        sensor_y = jnp.clip(local_y, 0, by - 1) + 8
        sensor_z = jnp.where(own, local_z, -1)
        smem = pl.BlockSpec(memory_space=pltpu.SMEM)
        hbm = pl.BlockSpec(memory_space=pl.ANY)
        vmem = pl.BlockSpec(memory_space=pltpu.VMEM)
        dma = pltpu.SemaphoreType.DMA
        block = jax.ShapeDtypeStruct((bx, by, bz), F32)
        outs = pl.pallas_call(
            functools.partial(kernel, (gx, gy, gz, nx, ny, nz)),
            out_shape=(
                block,
                block,
                block,
                jax.ShapeDtypeStruct((S // 128, 128), F32),
                jax.ShapeDtypeStruct((1,), F32),
            ),
            in_specs=[smem] * 5 + [hbm] * 7 + [vmem],
            out_specs=(hbm, hbm, hbm, vmem, smem),
            scratch_shapes=[
                pltpu.VMEM((2, kx_own, ky_own, nz), F32),
                pltpu.VMEM((2, kx_own, ky_own, nz), F32),
                pltpu.VMEM((kx_own * 2 * ky_own, nz), BF16),
                pltpu.VMEM((kx_own * 2 * ky_own, nz), BF16),
                pltpu.VMEM(depth.shape, BF16),
                pltpu.VMEM(first.shape, BF16),
                pltpu.VMEM(second.shape, BF16),
                pltpu.VMEM((CHUNKS, nd * part, kx_own, 128), F32),
                pltpu.VMEM((CHUNKS, part, nx, 128), F32),
                pltpu.VMEM((CHUNKS, part, nx, 128), F32),
                pltpu.VMEM((CHUNKS, gx, part, bx, 128), F32),
                pltpu.VMEM((CHUNKS, gy, part * bx // 2, 128), F32),
                pltpu.VMEM((bz * bx // 2, 128), F32),
                pltpu.VMEM((bx, by, bz), F32),
                pltpu.VMEM((2, 2, bx + 2, by + 16, bz), F32),
                pltpu.VMEM((STEPS, 2, 2, by, bz), F32),
                pltpu.VMEM((STEPS, 2, 2, by, bz), F32),
                pltpu.VMEM((STEPS, 2, 2, bx, bz), F32),
                pltpu.VMEM((STEPS, 2, 2, bx, bz), F32),
                pltpu.VMEM((STEPS, 2, by, bz), F32),
                pltpu.VMEM((STEPS, 2, by, bz), F32),
                pltpu.VMEM((S, 128), F32),
                pltpu.VMEM((gx, 8, 128), F32),
                pltpu.VMEM((gx, 8, 128), F32),
                pltpu.VMEM((8, 128), F32),
                pltpu.VMEM((nd, 8, 128), F32),
                pltpu.VMEM((8, 128), F32),
                pltpu.VMEM((gx, 8, 128), F32),
                dma((7,)),
                dma((3,)),
                dma((CHUNKS,)),
                dma((CHUNKS,)),
                dma((CHUNKS,)),
                dma((CHUNKS,)),
                dma((1,)),
                dma((1,)),
                dma((STEPS, 3, 2)),
                dma((STEPS, 3, 2)),
                dma((3,)),
                dma((3,)),
            ],
            compiler_params=pltpu.CompilerParams(
                collective_id=0, has_side_effects=True, vmem_limit_bytes=56 * 1024 * 1024
            ),
            cost_estimate=pl.CostEstimate(
                flops=7_000_000_000, bytes_accessed=16_000_000, transcendentals=1_000_000
            ),
        )(
            beta,
            sensor_x,
            sensor_y,
            sensor_z,
            cost,
            incumbent,
            renewed,
            jnp.asarray(depth),
            jnp.asarray(first),
            jnp.asarray(second),
            rho,
            heat,
            recorded.reshape(S // 128, 128),
        )
        energy, density, kelvin, model, odds = outs
        return energy, density, kelvin, model.reshape(S), odds

    return jax.shard_map(
        body,
        mesh=mesh,
        in_specs=(
            P(None, ("gy", "gz"), "gx", None),
            P(None, ("gy", "gz"), "gx", None),
            P(),
            P("gx", "gy", "gz"),
            P("gx", "gy", "gz"),
            P(),
            P(),
            P(),
        ),
        out_specs=(P("gx", "gy", "gz"), P("gx", "gy", "gz"), P("gx", "gy", "gz"), P(), P()),
        check_vma=False,
    )
```

```python
import functools
import math

import jax
import jax.numpy as jnp
import ml_dtypes
import numpy as np
from jax import lax
from jax.experimental import pallas as pl
from jax.experimental.pallas import tpu as pltpu
from jax.sharding import PartitionSpec as P

MESH_EXTENT_EAST = 256
MESH_EXTENT_NORTH = 512
MESH_EXTENT_UPWARD = 512
STEPS = 3
S = 4096
CHUNKS = 8
LAG = 3
GROUPS = 4
SLOTS = 8
ABL = set()
MESH = pl.DeviceIdType.MESH
F32 = jnp.float32
BF16 = jnp.bfloat16
NT = (((1,), (1,)), ((), ()))


def spectrum(length):
    wave = np.arange(length)
    signed = np.where(wave < length // 2, wave, wave - length).astype(np.float64)
    shape = 1.0 / np.sqrt(1.0 + (signed / 8.0) ** 2)
    return shape / np.sqrt(np.sum(shape * shape))


def waves(places, numbers, length):
    angle = (places[:, None] * numbers[None, :] % length) * (2.0 * math.pi / length)
    scale = spectrum(length)[numbers][None, :]
    return np.cos(angle) * scale, np.sin(angle) * scale


def halves(table):
    high = table.astype(np.float32).astype(ml_dtypes.bfloat16)
    low = (table - high.astype(np.float64)).astype(np.float32).astype(ml_dtypes.bfloat16)
    return high, low


def tables(gx, gy, gz, nx, ny, nz):
    sub = nz // (gy * gz)
    part = sub // CHUNKS
    stacks = []
    for chunk in range(CHUNKS):
        places = np.concatenate(
            [
                z * (nz // gz) + y * sub + chunk * part + np.arange(part)
                for y in range(gy)
                for z in range(gz)
            ]
        )
        cosine, sine = waves(places, np.arange(nz), nz)
        stacks.append(np.concatenate(halves(np.concatenate([cosine, sine]))))
    depth = np.stack(stacks)
    cosine, sine = waves(np.arange(nx), np.arange(nx), nx)
    first = np.concatenate(halves(np.concatenate([cosine, sine])))
    width = ny // gx
    blocks = []
    for block in range(gx):
        cosine, sine = waves(np.arange(ny), block * width + np.arange(width), ny)
        blocks += [cosine.T, -sine.T]
    second = np.stack(halves(np.concatenate(blocks)))
    return depth, first, second


def split(values):
    high = values.astype(BF16)
    return high, (values - high.astype(F32)).astype(BF16)


PLANE_ORDER = [
    (dx, dy, dc)
    for dx, dy in [
        (2, 2), (1, 0), (0, 1), (3, 0), (0, 3), (2, 1), (1, 2), (2, 3),
        (3, 2), (1, 1), (3, 3), (2, 0), (0, 2), (1, 3), (3, 1), (0, 0),
    ]
    for dc in range(2)
    if (dx, dy, dc) != (0, 0, 0)
]
LINE_ORDER = [4, 3, -3, 2, -2, 1, -1]
ROW_ORDER = [(2, 1), (1, 0), (3, 1), (2, 0), (1, 1), (3, 0), (0, 1)]


def places(gx, gy, gz):
    ix, iy, iz = lax.axis_index("gx"), lax.axis_index("gy"), lax.axis_index("gz")
    nx_ring = gy // 2
    x, y_high = lax.rem(iy, nx_ring), iy // nx_ring
    y, core = y_high * (gz // 2) + iz // 2, lax.rem(iz, 2)
    turn = 1 - 2 * core

    def plane(offset):
        dx, dy, dc = offset
        to_x = lax.rem(x + turn * dx + 2 * nx_ring, nx_ring)
        to_y = lax.rem(y + turn * dy + 2 * gz, gz)
        to_core = lax.rem(core + dc, 2)
        to = ((to_y // 2) * nx_ring + to_x, lax.rem(to_y, 2) * 2 + to_core)
        return to[0] * gz + to[1], (ix,) + to

    def line(k):
        other = lax.rem(ix + turn * k + 2 * gx, gx)
        return other, (other, iy, iz)

    def row(offset):
        dx, dy = offset
        other = lax.rem(y_high + dy, 2) * nx_ring + lax.rem(x + turn * dx + 2 * nx_ring, nx_ring)
        return other, (ix, other, iz)

    return (ix, iy, iz), plane, line, row


def greet(plane, line):
    barrier = pltpu.get_barrier_semaphore()
    for offset in PLANE_ORDER:
        pl.semaphore_signal(barrier, inc=1, device_id=plane(offset)[1], device_id_type=MESH)
    for offset in LINE_ORDER:
        pl.semaphore_signal(barrier, inc=1, device_id=line(offset)[1], device_id_type=MESH)


def met():
    pl.semaphore_wait(pltpu.get_barrier_semaphore(), len(PLANE_ORDER) + len(LINE_ORDER))


def remote(src, dst, send_sem, recv_sem, device):
    pltpu.make_async_remote_copy(
        src_ref=src,
        dst_ref=dst,
        send_sem=send_sem,
        recv_sem=recv_sem,
        device_id=device,
        device_id_type=MESH,
    ).start()


def settle(ref, sem):
    pltpu.make_async_copy(ref, ref, sem).wait()


def kernel(
    dims,
    beta,
    inc,
    ren,
    w1_hbm,
    w2_hbm,
    w3_hbm,
    rho0,
    heat0,
    sensors,
    thr_out,
    rho_out,
    heat_out,
    code_out,
    most_out,
    inc_v,
    ren_v,
    b_high,
    b_low,
    w1,
    w2,
    w3,
    send1,
    got1,
    send2,
    got2,
    send3,
    got3,
    thr,
    inverse,
    state,
    heat_last,
    rho_last,
    hy_send,
    hy_got,
    hz_send,
    hz_got,
    load_sem,
    out_sem,
    s1_sem,
    r1_sem,
    s2_sem,
    r2_sem,
    s3_sem,
    r3_sem,
    hxs_sem,
    hxr_sem,
    hs_sem,
    hr_sem,
):
    gx, gy, gz, nx, ny, nz = dims
    nd = gy * gz
    sub = nz // nd
    part = sub // CHUNKS
    bx, by, bz = nx // gx, ny // gy, nz // gz
    half = bx // 2
    kx_own = nx // nd
    (ix, iy, iz), plane_device, line_device, row_device = places(gx, gy, gz)
    me = iy * gz + iz
    middle = pl.ds(8, by)

    loads = [
        pltpu.make_async_copy(inc, inc_v, load_sem.at[0]),
        pltpu.make_async_copy(ren, ren_v, load_sem.at[1]),
        pltpu.make_async_copy(w1_hbm, w1, load_sem.at[2]),
        pltpu.make_async_copy(heat0, state.at[0, 0, pl.ds(1, bx), middle, :], load_sem.at[3]),
        pltpu.make_async_copy(rho0, state.at[0, 1, pl.ds(1, bx), middle, :], load_sem.at[4]),
        pltpu.make_async_copy(w2_hbm, w2, load_sem.at[5]),
        pltpu.make_async_copy(w3_hbm, w3, load_sem.at[6]),
    ]
    for load in loads:
        load.start()
    greet(plane_device, line_device)

    lane = lax.broadcasted_iota(jnp.int32, (1, 128), 1)
    sign = jnp.where(lane < 64, -1.0, 1.0).astype(F32)
    first_half = lane < 64

    loads[0].wait()
    loads[1].wait()
    weight = jnp.full((1, 128), beta[0], F32)
    keep = jnp.sqrt(1.0 - weight * weight)[:, :1]
    fresh = weight[:, :1]

    def mix(k, carry):
        for part_of in range(2):
            mixed = keep * inc_v[part_of, k] + fresh * ren_v[part_of, k]
            high, low = split(mixed)
            rows = pl.ds(pl.multiple_of(k * 128 + part_of * 64, 64), 64)
            b_high[rows, :] = high
            b_low[rows, :] = low
        return carry

    lax.fori_loop(0, kx_own, mix, 0)
    loads[2].wait()

    rows1 = nd * part

    def stage1(c):
        flat = send1.at[c].reshape(rows1 * kx_own, 128)
        for q in range(kx_own // 2):
            right = pl.ds(q * 256, 256)
            top = lax.dot_general(w1[c], b_high[right, :], NT, preferred_element_type=F32)
            low = lax.dot_general(
                w1[c, pl.ds(0, 2 * rows1), :], b_low[right, :], NT, preferred_element_type=F32
            )
            total = top[: 2 * rows1] + top[2 * rows1 :] + low
            for side in range(2):
                cut = slice(side * 128, side * 128 + 128)
                cosines = total[:rows1, cut]
                sines = total[rows1:, cut]
                flat[pl.ds(2 * q + side, rows1, stride=kx_own), :] = cosines + sign * pltpu.roll(
                    sines, 64, 1
                )

    def ship1(c):
        for offset in PLANE_ORDER:
            other, device = plane_device(offset)
            remote(
                send1.at[c, pl.ds(other * part, part)],
                got1.at[c, me],
                s1_sem.at[c],
                r1_sem.at[c],
                device,
            )
        pltpu.make_async_copy(
            send1.at[c, pl.ds(me * part, part)], got1.at[c, me], r1_sem.at[c]
        ).start()

    def stage2(c):
        settle(got1.at[c], r1_sem.at[c])
        for p in range(part // 2):
            values = jnp.concatenate(
                [got1[c, :, 2 * p + side].reshape(nx, 128) for side in range(2)], axis=1
            )
            high, low = split(values)
            top = jnp.dot(w2[...], high, preferred_element_type=F32)
            bottom = jnp.dot(w2[pl.ds(0, 2 * nx), :], low, preferred_element_type=F32)
            total = top[: 2 * nx] + top[2 * nx :] + bottom
            for side in range(2):
                cut = slice(side * 128, side * 128 + 128)
                result = total[:nx, cut] + sign * pltpu.roll(total[nx:, cut], 64, 1)
                send2[c, :, 2 * p + side] = result.reshape(gx, bx, 128)
        for k in LINE_ORDER:
            other, device = line_device(k)
            remote(send2.at[c, other], got2.at[c, ix], s2_sem.at[c], r2_sem.at[c], device)
        pltpu.make_async_copy(send2.at[c, ix], got2.at[c, ix], r2_sem.at[c]).start()

    def stage3(c):
        settle(got2.at[c], r2_sem.at[c])
        rows = part * bx
        values = jnp.concatenate([got2[c, g].reshape(rows, 128) for g in range(gx)], axis=1)
        high, low = split(values)
        both = jnp.concatenate([high, low], axis=0)
        for t in range(ny // 256):
            columns = pl.ds(t * 256, 256)
            top = jnp.dot(both, w3[0, :, columns], preferred_element_type=F32)
            field = (
                top[:rows]
                + top[rows:]
                + jnp.dot(high, w3[1, :, columns], preferred_element_type=F32)
            )
            energy = 2.0 + 0.6 * jnp.tanh(field)
            for side in range(2):
                tile = energy[:, side * 128 : side * 128 + 128].reshape(part, 2, half, 128)
                near = tile[:, 0].reshape(part * half, 128)
                far = tile[:, 1].reshape(part * half, 128)
                j = 4 * t + 2 * side
                send3[c, j] = jnp.where(first_half, near, pltpu.roll(far, 64, 1))
                send3[c, j + 1] = jnp.where(first_half, pltpu.roll(near, 64, 1), far)
        target = got3.at[
            pl.ds(pl.multiple_of((iy * sub + c * part) * half, part * half), part * half), :
        ]
        for offset in ROW_ORDER:
            other, device = row_device(offset)
            remote(send3.at[c, other], target, s3_sem.at[0], r3_sem.at[0], device)
        pltpu.make_async_copy(send3.at[c, iy], target, r3_sem.at[0]).start()

    def spot(g, slot):
        return lax.rem(g * SLOTS + slot + bx - 1, bx)

    near_ones = []
    for number, (place, count) in enumerate([(ix, gx), (iy, gy), (iz, gz)]):
        for end in range(2):
            device = [ix, iy, iz]
            device[number] = place + (-1 if end == 0 else 1)
            inner = place > 0 if end == 0 else place < count - 1
            near_ones.append((number, end, inner, tuple(device)))

    outside = jnp.where(lax.rem(lane, 4) < 2, 1.25, 0.0).astype(F32)
    for number, end, inner, device in near_ones:

        @pl.when(jnp.logical_not(inner))
        def _(number=number, end=end):
            for level in range(STEPS):
                if number == 0:
                    x = 0 if end == 0 else bx + 1
                    state[level, 0, x, middle, :] = jnp.full((by, bz), 1.25, F32)
                    state[level, 1, x, middle, :] = jnp.zeros((by, bz), F32)
                elif number == 1:
                    shape = (GROUPS, 1, SLOTS, bz)
                    hy_got[level, end, :, pl.ds(0, 1)] = jnp.full(shape, 1.25, F32)
                    hy_got[level, end, :, pl.ds(1, 1)] = jnp.zeros(shape, F32)
                else:
                    hz_got[level, end] = jnp.broadcast_to(outside, (GROUPS, by, 128))

    def offer(level, g):
        packed = jnp.zeros((by, 128), F32)
        for slot in range(SLOTS):
            x = spot(g, slot) + 1
            heat = state[level, 0, x, middle, :]
            rho = state[level, 1, x, middle, :]
            for f, values in ((0, heat), (1, rho)):
                hy_send[level, 0, g, f, pl.ds(slot, 1), :] = values[:1]
                hy_send[level, 1, g, f, pl.ds(slot, 1), :] = values[by - 1 :]
            ends = jnp.where(lane < 2, pltpu.roll(heat, 1, 1), pltpu.roll(rho, 3, 1))
            if slot:
                ends = pltpu.roll(ends, 4 * slot, 1)
            packed = jnp.where(lane // 4 == slot, ends, packed)
        hz_send[level, g] = packed
        for number, end, inner, device in near_ones:
            if number == 0:
                continue

            @pl.when(inner)
            def _(number=number, end=end, device=device):
                src = hy_send.at[level, end, g] if number == 1 else hz_send.at[level, g]
                dst = (hy_got if number == 1 else hz_got).at[level, 1 - end, g]
                remote(
                    src,
                    dst,
                    hs_sem.at[level, number - 1, end, g],
                    hr_sem.at[level, number - 1, 1 - end, g],
                    device,
                )

    def offer_ends(level):
        for number, end, inner, device in near_ones[:2]:

            @pl.when(inner)
            def _(end=end, device=device):
                remote(
                    state.at[level, :, 1 if end == 0 else bx, middle, :],
                    state.at[level, :, bx + 1 if end == 0 else 0, middle, :],
                    hxs_sem.at[level, end],
                    hxr_sem.at[level, 1 - end],
                    device,
                )

    def accept_ends(level):
        for number, end, inner, device in near_ones[:2]:

            @pl.when(inner)
            def _(end=end):
                settle(
                    state.at[level, :, 0 if end == 0 else bx + 1, middle, :],
                    hxr_sem.at[level, end],
                )

    def accept(level, g):
        for number, end, inner, device in near_ones[2:]:

            @pl.when(inner)
            def _(number=number, end=end):
                settle(
                    (hy_got if number == 1 else hz_got).at[level, end, g],
                    hr_sem.at[level, number - 1, end, g],
                )

        for slot in range(SLOTS):
            x = spot(g, slot) + 1
            for f in range(2):
                row = pl.ds(slot, 1)
                state[level, f, x, pl.ds(7, 1), :] = hy_got[level, 0, g, f, row, :]
                state[level, f, x, pl.ds(8 + by, 1), :] = hy_got[level, 1, g, f, row, :]

    def flux_of(level, g, slot):
        x = spot(g, slot) + 1

        def at(f, dx, dy):
            return state[level, f, x + dx, pl.ds(8 + dy, by), :]

        heat, rho = at(0, 0, 0), at(1, 0, 0)
        cond = rho * rho
        around = [(at(0, dx, dy), at(1, dx, dy)) for dx, dy in ((1, 0), (-1, 0), (0, 1), (0, -1))]
        for end in range(2):
            packed = hz_got[level, end, g]
            edge = 0 if end == 0 else 127
            turn = 1 if end == 0 else 127
            pair = []
            for f, values in ((0, heat), (1, rho)):
                shift = (edge - (4 * slot + 2 * f + end)) % 128
                beyond = pltpu.roll(packed, shift, 1) if shift else packed
                pair.append(jnp.where(lane == edge, beyond, pltpu.roll(values, turn, 1)))
            around.append(tuple(pair))
        flux = None
        for heat_side, rho_side in around:
            term = (cond + rho_side * rho_side) * (heat_side - heat)
            flux = term if flux is None else flux + term
        return x, heat, rho, flux

    def prepare(g, carry):
        accept(0, g)
        for slot in range(SLOTS):
            x, heat, rho, flux = flux_of(0, g, slot)
            state[1, 0, x, middle, :] = heat + 0.08 * flux
            inverse[x - 1] = -1.0 / heat
        return carry

    def first_step(g, carry):
        for slot in range(SLOTS):
            x = spot(g, slot)
            rho = state[0, 1, x + 1, middle, :]
            growth = jnp.exp(thr[x] * inverse[x]) * (1.0 - rho)
            state[1, 0, x + 1, middle, :] = state[1, 0, x + 1, middle, :] + 0.48 * growth
            state[1, 1, x + 1, middle, :] = rho + 0.64 * growth
        offer(1, g)

        @pl.when(g == 0)
        def _():
            offer_ends(1)

        return carry

    def later_step(level):
        def group(g, carry):
            @pl.when(g == 0)
            def _():
                accept_ends(level)

            accept(level, g)
            for slot in range(SLOTS):
                x, heat, rho, flux = flux_of(level, g, slot)
                growth = jnp.exp(-thr[x - 1] / heat) * (1.0 - rho)
                new_heat = heat + 0.16 * (0.5 * flux + 3.0 * growth)
                new_rho = rho + 0.64 * growth
                if level + 1 < STEPS:
                    state[level + 1, 0, x, middle, :] = new_heat
                    state[level + 1, 1, x, middle, :] = new_rho
                else:
                    heat_last[x - 1] = new_heat
                    rho_last[x - 1] = new_rho
            if level + 1 < STEPS:
                offer(level + 1, g)

                @pl.when(g == 0)
                def _():
                    offer_ends(level + 1)

            return carry

        lax.fori_loop(0, GROUPS, group, 0)

    def offer_first(g, carry):
        offer(0, g)
        return carry

    def locate():
        x = sensors[0:1, :] - ix * bx
        y = sensors[1:2, :] - iy * by
        z = sensors[2:3, :] - iz * bz
        own = (x >= 0) & (x < bx) & (y >= 0) & (y < by) & (z >= 0) & (z < bz)
        code = jnp.where(own, (x * by + y) * bz + z, -1)
        code_out[...] = code
        width = most_out.shape[1]
        most = code[:, :width]
        for k in range(1, S // width):
            most = jnp.maximum(most, code[:, k * width : (k + 1) * width])
        most_out[...] = most

    stage1(0)
    met()

    def pipeline(i, carry):
        @pl.when((i > 0) & (i < CHUNKS))
        def _():
            stage1(i)

        @pl.when(i < CHUNKS)
        def _():
            ship1(i)

        @pl.when(i == 0)
        def _():
            loads[3].wait()
            loads[4].wait()
            offer_ends(0)
            lax.fori_loop(0, GROUPS, offer_first, 0)
            loads[5].wait()
            loads[6].wait()

        @pl.when((i >= 1) & (i <= CHUNKS))
        def _():
            stage2(i - 1)

        @pl.when(i == 2)
        def _():
            locate()
            accept_ends(0)

        @pl.when((i >= 2) & (i < 2 + GROUPS))
        def _():
            prepare(i - 2, 0)

        @pl.when(i >= LAG)
        def _():
            stage3(i - LAG)

        return carry

    lax.fori_loop(0, CHUNKS + LAG, pipeline, 0)

    settle(got3, r3_sem.at[0])
    for x in range(half):
        turned = got3[pl.ds(x, bz, stride=half), :].T
        thr[x] = turned[:by]
        thr[half + x] = turned[by:]
    thr_copy = pltpu.make_async_copy(thr, thr_out, out_sem.at[0])
    thr_copy.start()

    lax.fori_loop(0, GROUPS, first_step, 0)
    for level in range(1, STEPS):
        later_step(level)
    heat_copy = pltpu.make_async_copy(heat_last, heat_out, out_sem.at[1])
    rho_copy = pltpu.make_async_copy(rho_last, rho_out, out_sem.at[2])
    heat_copy.start()
    rho_copy.start()

    def drain_chunk(c, carry):
        settle(send1.at[c, pl.ds(0, (nd - 1) * part)], s1_sem.at[c])
        settle(send2.at[c, pl.ds(0, gx - 1)], s2_sem.at[c])
        return carry

    lax.fori_loop(0, CHUNKS, drain_chunk, 0)
    settle(send3.at[:, pl.ds(0, gy - 1)], s3_sem.at[0])
    for number, end, inner, device in near_ones:

        @pl.when(inner)
        def _(number=number, end=end):
            for level in range(STEPS):
                if number == 0:
                    settle(
                        state.at[level, :, 1 if end == 0 else bx, middle, :],
                        hxs_sem.at[level, end],
                    )
                    continue
                for g in range(GROUPS):
                    settle(
                        hy_send.at[level, end, g] if number == 1 else hz_send.at[level, g],
                        hs_sem.at[level, number - 1, end, g],
                    )

    thr_copy.wait()
    heat_copy.wait()
    rho_copy.wait()


def read_kernel(
    by, code, most, thr, rho, heat, thr_out, rho_out, heat_out, found, thr_v, rho_v, heat_v, sem
):
    ins = [
        pltpu.make_async_copy(src, dst, sem.at[k])
        for k, (src, dst) in enumerate(((heat, heat_v), (thr, thr_v), (rho, rho_v)))
    ]
    outs = [
        pltpu.make_async_copy(src, dst, sem.at[3 + k])
        for k, (src, dst) in enumerate(((heat_v, heat_out), (thr_v, thr_out), (rho_v, rho_out)))
    ]
    for copy in ins:
        copy.start()
    found[...] = jnp.zeros(found.shape, F32)
    for copy, after in zip(ins, outs):
        copy.wait()
        after.start()
    lane = lax.broadcasted_iota(jnp.int32, (1, 128), 1)
    width = most.shape[1]

    def column(j, carry):
        @pl.when(most[0, j] >= 0)
        def _():
            def one(k, carry):
                s = k * width + j
                cell = code[0, s]

                @pl.when(cell >= 0)
                def _():
                    row = heat_v[cell // (128 * by), pl.ds(lax.rem(cell // 128, by), 1), :]
                    where = lax.rem(s, 128)
                    turned = pltpu.roll(row, lax.rem(where - lax.rem(cell, 128) + 128, 128), 1)
                    target = pl.ds(s // 512 * 8 + lax.rem(s // 128, 4), 1)
                    found[target, :] = jnp.where(lane == where, turned, found[target, :])

                return carry

            lax.fori_loop(0, S // width, one, 0)

        return carry

    lax.fori_loop(0, width, column, 0)
    for copy in outs:
        copy.wait()


def sum_kernel(
    dims, cost, found, recorded, model_out, odds_out, send, red_a, red_mid, red_b, red_fin, red_c,
    rs_sem, rr_sem,
):
    gx, gy, gz = dims
    (ix, iy, iz), plane_device, line_device, _ = places(gx, gy, gz)
    me = iy * gz + iz
    per = S // 128 // gx
    greet(plane_device, line_device)
    for block in range(gx):
        send[block] = found[pl.ds(block * 8, 8), :]
    met()
    for k in LINE_ORDER:
        other, device = line_device(k)
        remote(send.at[other], red_a.at[ix], rs_sem.at[0], rr_sem.at[0], device)
    pltpu.make_async_copy(send.at[ix], red_a.at[ix], rr_sem.at[0]).start()
    settle(red_a, rr_sem.at[0])
    red_mid[...] = jnp.sum(red_a[...], axis=0)
    for offset in PLANE_ORDER:
        remote(red_mid, red_b.at[me], rs_sem.at[1], rr_sem.at[1], plane_device(offset)[1])
    pltpu.make_async_copy(red_mid, red_b.at[me], rr_sem.at[1]).start()
    settle(red_b, rr_sem.at[1])
    red_fin[...] = jnp.sum(red_b[...], axis=0)
    for k in LINE_ORDER:
        remote(red_fin, red_c.at[ix], rs_sem.at[2], rr_sem.at[2], line_device(k)[1])
    pltpu.make_async_copy(red_fin, red_c.at[ix], rr_sem.at[2]).start()
    settle(red_c, rr_sem.at[2])
    misfit = jnp.zeros((per, 128), F32)
    for block in range(gx):
        values = red_c[block, pl.ds(0, per), :]
        model_out[pl.ds(block * per, per), :] = values
        gap = (values - recorded[pl.ds(block * per, per), :]) / 0.2
        misfit = misfit + gap * gap
    odds_out[0] = cost[0] - 0.5 * (jnp.sum(misfit) / S)
    settle(red_a.at[pl.ds(0, gx - 1)], rs_sem.at[0])
    settle(red_b.at[pl.ds(0, gy * gz - 1)], rs_sem.at[1])
    settle(red_c.at[pl.ds(0, gx - 1)], rs_sem.at[2])


def solution(mesh):
    gx, gy, gz = (mesh.shape[name] for name in ("gx", "gy", "gz"))
    nx, ny, nz = MESH_EXTENT_EAST, MESH_EXTENT_NORTH, MESH_EXTENT_UPWARD
    depth, first, second = tables(gx, gy, gz, nx, ny, nz)
    nd = gy * gz
    sub = nz // nd
    part = sub // CHUNKS
    bx, by, bz = nx // gx, ny // gy, nz // gz
    kx_own, ky_own = nx // nd, ny // gx
    smem = pl.BlockSpec(memory_space=pltpu.SMEM)
    hbm = pl.BlockSpec(memory_space=pl.ANY)
    vmem = pl.BlockSpec(memory_space=pltpu.VMEM)
    dma = pltpu.SemaphoreType.DMA
    block = jax.ShapeDtypeStruct((bx, by, bz), F32)

    def body(incumbent, renewed, beta, rho, heat, place, recorded, cost):
        energy, density, kelvin, code, most = pl.pallas_call(
            functools.partial(kernel, (gx, gy, gz, nx, ny, nz)),
            out_shape=(
                block,
                block,
                block,
                jax.ShapeDtypeStruct((1, S), jnp.int32),
                jax.ShapeDtypeStruct((1, 256), jnp.int32),
            ),
            in_specs=[smem] + [hbm] * 7 + [vmem],
            out_specs=(hbm, hbm, hbm, vmem, vmem),
            scratch_shapes=[
                pltpu.VMEM((2, kx_own, ky_own, nz), F32),
                pltpu.VMEM((2, kx_own, ky_own, nz), F32),
                pltpu.VMEM((kx_own * 2 * ky_own, nz), BF16),
                pltpu.VMEM((kx_own * 2 * ky_own, nz), BF16),
                pltpu.VMEM(depth.shape, BF16),
                pltpu.VMEM(first.shape, BF16),
                pltpu.VMEM(second.shape, BF16),
                pltpu.VMEM((CHUNKS, nd * part, kx_own, 128), F32),
                pltpu.VMEM((CHUNKS, nd, part, kx_own, 128), F32),
                pltpu.VMEM((CHUNKS, gx, part, bx, 128), F32),
                pltpu.VMEM((CHUNKS, gx, part, bx, 128), F32),
                pltpu.VMEM((CHUNKS, gy, part * bx // 2, 128), F32),
                pltpu.VMEM((bz * bx // 2, 128), F32),
                pltpu.VMEM((bx, by, bz), F32),
                pltpu.VMEM((bx, by, bz), F32),
                pltpu.VMEM((STEPS, 2, bx + 2, by + 16, bz), F32),
                pltpu.VMEM((bx, by, bz), F32),
                pltpu.VMEM((bx, by, bz), F32),
                pltpu.VMEM((STEPS, 2, GROUPS, 2, SLOTS, bz), F32),
                pltpu.VMEM((STEPS, 2, GROUPS, 2, SLOTS, bz), F32),
                pltpu.VMEM((STEPS, GROUPS, by, bz), F32),
                pltpu.VMEM((STEPS, 2, GROUPS, by, bz), F32),
                dma((7,)),
                dma((3,)),
                dma((CHUNKS,)),
                dma((CHUNKS,)),
                dma((CHUNKS,)),
                dma((CHUNKS,)),
                dma((1,)),
                dma((1,)),
                dma((STEPS, 2)),
                dma((STEPS, 2)),
                dma((STEPS, 2, 2, GROUPS)),
                dma((STEPS, 2, 2, GROUPS)),
            ],
            compiler_params=pltpu.CompilerParams(
                collective_id=0, has_side_effects=True, vmem_limit_bytes=56 * 1024 * 1024
            ),
            cost_estimate=pl.CostEstimate(
                flops=7_000_000_000, bytes_accessed=16_000_000, transcendentals=1_000_000
            ),
        )(
            beta,
            incumbent,
            renewed,
            jnp.asarray(depth),
            jnp.asarray(first),
            jnp.asarray(second),
            rho,
            heat,
            place.T,
        )
        energy, density, kelvin, found = pl.pallas_call(
            functools.partial(read_kernel, by),
            out_shape=(block, block, block, jax.ShapeDtypeStruct((gx * 8, 128), F32)),
            in_specs=[smem] * 2 + [hbm] * 3,
            out_specs=(hbm, hbm, hbm, vmem),
            scratch_shapes=[pltpu.VMEM((bx, by, bz), F32)] * 3 + [dma((6,))],
            compiler_params=pltpu.CompilerParams(vmem_limit_bytes=16 * 1024 * 1024),
        )(code, most, energy, density, kelvin)
        model, odds = pl.pallas_call(
            functools.partial(sum_kernel, (gx, gy, gz)),
            out_shape=(
                jax.ShapeDtypeStruct((S // 128, 128), F32),
                jax.ShapeDtypeStruct((1,), F32),
            ),
            in_specs=[smem, vmem, vmem],
            out_specs=(vmem, smem),
            scratch_shapes=[
                pltpu.VMEM((gx, 8, 128), F32),
                pltpu.VMEM((gx, 8, 128), F32),
                pltpu.VMEM((8, 128), F32),
                pltpu.VMEM((nd, 8, 128), F32),
                pltpu.VMEM((8, 128), F32),
                pltpu.VMEM((gx, 8, 128), F32),
                dma((3,)),
                dma((3,)),
            ],
            compiler_params=pltpu.CompilerParams(collective_id=1, has_side_effects=True),
        )(cost, found, recorded.reshape(S // 128, 128))
        return energy, density, kelvin, model.reshape(S), odds

    return jax.shard_map(
        body,
        mesh=mesh,
        in_specs=(
            P(None, ("gy", "gz"), "gx", None),
            P(None, ("gy", "gz"), "gx", None),
            P(),
            P("gx", "gy", "gz"),
            P("gx", "gy", "gz"),
            P(),
            P(),
            P(),
        ),
        out_specs=(P("gx", "gy", "gz"), P("gx", "gy", "gz"), P("gx", "gy", "gz"), P(), P()),
        check_vma=False,
    )
```

```python
import functools
import math

import jax
import jax.numpy as jnp
import ml_dtypes
import numpy as np
from jax import lax
from jax.experimental import pallas as pl
from jax.experimental.pallas import tpu as pltpu
from jax.sharding import PartitionSpec as P

MESH_EXTENT_EAST = 256
MESH_EXTENT_NORTH = 512
MESH_EXTENT_UPWARD = 512
STEPS = 3
S = 4096
CHUNKS = 8
LAG = 3
GROUPS = 4
SLOTS = 8
PIECE = 32
ABL = set()
MESH = pl.DeviceIdType.MESH
F32 = jnp.float32
BF16 = jnp.bfloat16
NT = (((1,), (1,)), ((), ()))


def spectrum(length):
    wave = np.arange(length)
    signed = np.where(wave < length // 2, wave, wave - length).astype(np.float64)
    shape = 1.0 / np.sqrt(1.0 + (signed / 8.0) ** 2)
    return shape / np.sqrt(np.sum(shape * shape))


def waves(places, numbers, length):
    angle = (places[:, None] * numbers[None, :] % length) * (2.0 * math.pi / length)
    scale = spectrum(length)[numbers][None, :]
    return np.cos(angle) * scale, np.sin(angle) * scale


def halves(table):
    high = table.astype(np.float32).astype(ml_dtypes.bfloat16)
    low = (table - high.astype(np.float64)).astype(np.float32).astype(ml_dtypes.bfloat16)
    return high, low


def tables(gx, gy, gz, nx, ny, nz):
    sub = nz // (gy * gz)
    part = sub // CHUNKS
    stacks = []
    for chunk in range(CHUNKS):
        places = np.concatenate(
            [
                z * (nz // gz) + y * sub + chunk * part + np.arange(part)
                for y in range(gy)
                for z in range(gz)
            ]
        )
        cosine, sine = waves(places, np.arange(nz), nz)
        stacks.append(np.concatenate(halves(np.concatenate([cosine, sine]))))
    depth = np.stack(stacks)
    cosine, sine = waves(np.arange(nx), np.arange(nx), nx)
    first = np.concatenate(halves(np.concatenate([cosine, sine])))
    width = ny // gx
    blocks = []
    for block in range(gx):
        cosine, sine = waves(np.arange(ny), block * width + np.arange(width), ny)
        blocks += [cosine.T, -sine.T]
    second = np.stack(halves(np.concatenate(blocks)))
    return depth, first, second


def split(values):
    high = values.astype(BF16)
    return high, (values - high.astype(F32)).astype(BF16)


PLANE_ORDER = [
    (dx, dy, dc)
    for dx, dy in [
        (2, 2), (1, 0), (0, 1), (3, 0), (0, 3), (2, 1), (1, 2), (2, 3),
        (3, 2), (1, 1), (3, 3), (2, 0), (0, 2), (1, 3), (3, 1), (0, 0),
    ]
    for dc in range(2)
    if (dx, dy, dc) != (0, 0, 0)
]
LINE_ORDER = [4, 3, -3, 2, -2, 1, -1]
ROW_ORDER = [(2, 1), (1, 0), (3, 1), (2, 0), (1, 1), (3, 0), (0, 1)]


def places(gx, gy, gz):
    ix, iy, iz = lax.axis_index("gx"), lax.axis_index("gy"), lax.axis_index("gz")
    nx_ring = gy // 2
    x, y_high = lax.rem(iy, nx_ring), iy // nx_ring
    y, core = y_high * (gz // 2) + iz // 2, lax.rem(iz, 2)
    turn = 1 - 2 * core

    def plane(offset):
        dx, dy, dc = offset
        to_x = lax.rem(x + turn * dx + 2 * nx_ring, nx_ring)
        to_y = lax.rem(y + turn * dy + 2 * gz, gz)
        to_core = lax.rem(core + dc, 2)
        to = ((to_y // 2) * nx_ring + to_x, lax.rem(to_y, 2) * 2 + to_core)
        return to[0] * gz + to[1], (ix,) + to

    def line(k):
        other = lax.rem(ix + turn * k + 2 * gx, gx)
        return other, (other, iy, iz)

    def row(offset):
        dx, dy = offset
        other = lax.rem(y_high + dy, 2) * nx_ring + lax.rem(x + turn * dx + 2 * nx_ring, nx_ring)
        return other, (ix, other, iz)

    return (ix, iy, iz), plane, line, row


def greet(plane, line):
    barrier = pltpu.get_barrier_semaphore()
    for offset in PLANE_ORDER:
        pl.semaphore_signal(barrier, inc=1, device_id=plane(offset)[1], device_id_type=MESH)
    for offset in LINE_ORDER:
        pl.semaphore_signal(barrier, inc=1, device_id=line(offset)[1], device_id_type=MESH)


def met():
    pl.semaphore_wait(pltpu.get_barrier_semaphore(), len(PLANE_ORDER) + len(LINE_ORDER))


def remote(src, dst, send_sem, recv_sem, device):
    pltpu.make_async_remote_copy(
        src_ref=src,
        dst_ref=dst,
        send_sem=send_sem,
        recv_sem=recv_sem,
        device_id=device,
        device_id_type=MESH,
    ).start()


def settle(ref, sem):
    pltpu.make_async_copy(ref, ref, sem).wait()


def kernel(
    dims,
    beta,
    inc,
    ren,
    w1_hbm,
    w2_hbm,
    w3_hbm,
    rho0,
    heat0,
    sensors,
    thr_out,
    rho_out,
    heat_out,
    code_out,
    inc_v,
    ren_v,
    b_high,
    b_low,
    w1,
    w2,
    w3,
    send1,
    got1,
    send2,
    got2,
    send3,
    got3,
    thr,
    inverse,
    state,
    heat_last,
    rho_v,
    hy_send,
    hy_got,
    hz_send,
    hz_got,
    load_sem,
    out_sem,
    s1_sem,
    r1_sem,
    s2_sem,
    r2_sem,
    s3_sem,
    r3_sem,
    hxs_sem,
    hxr_sem,
    hs_sem,
    hr_sem,
):
    gx, gy, gz, nx, ny, nz = dims
    nd = gy * gz
    sub = nz // nd
    part = sub // CHUNKS
    bx, by, bz = nx // gx, ny // gy, nz // gz
    half = bx // 2
    kx_own = nx // nd
    (ix, iy, iz), plane_device, line_device, row_device = places(gx, gy, gz)
    me = iy * gz + iz
    middle = pl.ds(8, by)

    loads = [
        pltpu.make_async_copy(inc, inc_v, load_sem.at[0]),
        pltpu.make_async_copy(ren, ren_v, load_sem.at[1]),
        pltpu.make_async_copy(w1_hbm, w1, load_sem.at[2]),
        pltpu.make_async_copy(heat0, state.at[0, 0, pl.ds(1, bx), middle, :], load_sem.at[3]),
        pltpu.make_async_copy(rho0, rho_v, load_sem.at[4]),
        pltpu.make_async_copy(w2_hbm, w2, load_sem.at[5]),
        pltpu.make_async_copy(w3_hbm, w3, load_sem.at[6]),
    ]
    for load in loads:
        load.start()
    greet(plane_device, line_device)

    lane = lax.broadcasted_iota(jnp.int32, (1, 128), 1)
    sign = jnp.where(lane < 64, -1.0, 1.0).astype(F32)
    first_half = lane < 64

    loads[0].wait()
    loads[1].wait()
    weight = jnp.full((1, 128), beta[0], F32)
    keep = jnp.sqrt(1.0 - weight * weight)[:, :1]
    fresh = weight[:, :1]

    def mix(k, carry):
        for part_of in range(2):
            mixed = keep * inc_v[part_of, k] + fresh * ren_v[part_of, k]
            high, low = split(mixed)
            rows = pl.ds(pl.multiple_of(k * 128 + part_of * 64, 64), 64)
            b_high[rows, :] = high
            b_low[rows, :] = low
        return carry

    lax.fori_loop(0, kx_own, mix, 0)
    loads[2].wait()

    rows1 = nd * part

    def stage1(c):
        flat = send1.at[c].reshape(rows1 * kx_own, 128)
        for q in range(kx_own // 2):
            right = pl.ds(q * 256, 256)
            top = lax.dot_general(w1[c], b_high[right, :], NT, preferred_element_type=F32)
            low = lax.dot_general(
                w1[c, pl.ds(0, 2 * rows1), :], b_low[right, :], NT, preferred_element_type=F32
            )
            total = top[: 2 * rows1] + top[2 * rows1 :] + low
            for side in range(2):
                cut = slice(side * 128, side * 128 + 128)
                cosines = total[:rows1, cut]
                sines = total[rows1:, cut]
                flat[pl.ds(2 * q + side, rows1, stride=kx_own), :] = cosines + sign * pltpu.roll(
                    sines, 64, 1
                )

    def ship1(c):
        for offset in PLANE_ORDER:
            other, device = plane_device(offset)
            remote(
                send1.at[c, pl.ds(other * part, part)],
                got1.at[c, me],
                s1_sem.at[c],
                r1_sem.at[c],
                device,
            )
        pltpu.make_async_copy(
            send1.at[c, pl.ds(me * part, part)], got1.at[c, me], r1_sem.at[c]
        ).start()

    def stage2(c):
        settle(got1.at[c], r1_sem.at[c])
        for p in range(part // 2):
            values = jnp.concatenate(
                [got1[c, :, 2 * p + side].reshape(nx, 128) for side in range(2)], axis=1
            )
            high, low = split(values)
            top = jnp.dot(w2[...], high, preferred_element_type=F32)
            bottom = jnp.dot(w2[pl.ds(0, 2 * nx), :], low, preferred_element_type=F32)
            total = top[: 2 * nx] + top[2 * nx :] + bottom
            for side in range(2):
                cut = slice(side * 128, side * 128 + 128)
                result = total[:nx, cut] + sign * pltpu.roll(total[nx:, cut], 64, 1)
                send2[c, :, 2 * p + side] = result.reshape(gx, bx, 128)
        for k in LINE_ORDER:
            other, device = line_device(k)
            remote(send2.at[c, other], got2.at[c, ix], s2_sem.at[c], r2_sem.at[c], device)
        pltpu.make_async_copy(send2.at[c, ix], got2.at[c, ix], r2_sem.at[c]).start()

    def stage3(c):
        settle(got2.at[c], r2_sem.at[c])
        rows = part * bx
        values = jnp.concatenate([got2[c, g].reshape(rows, 128) for g in range(gx)], axis=1)
        high, low = split(values)
        both = jnp.concatenate([high, low], axis=0)
        for t in range(ny // 256):
            columns = pl.ds(t * 256, 256)
            top = jnp.dot(both, w3[0, :, columns], preferred_element_type=F32)
            field = (
                top[:rows]
                + top[rows:]
                + jnp.dot(high, w3[1, :, columns], preferred_element_type=F32)
            )
            energy = 2.0 + 0.6 * jnp.tanh(field)
            for side in range(2):
                tile = energy[:, side * 128 : side * 128 + 128].reshape(part, 2, half, 128)
                near = tile[:, 0].reshape(part * half, 128)
                far = tile[:, 1].reshape(part * half, 128)
                j = 4 * t + 2 * side
                send3[c, j] = jnp.where(first_half, near, pltpu.roll(far, 64, 1))
                send3[c, j + 1] = jnp.where(first_half, pltpu.roll(near, 64, 1), far)
        target = got3.at[
            pl.ds(pl.multiple_of((iy * sub + c * part) * half, part * half), part * half), :
        ]
        for offset in ROW_ORDER:
            other, device = row_device(offset)
            remote(send3.at[c, other], target, s3_sem.at[0], r3_sem.at[0], device)
        pltpu.make_async_copy(send3.at[c, iy], target, r3_sem.at[0]).start()

    def spot(g, slot):
        return lax.rem(g * SLOTS + slot + bx - 1, bx)

    near_ones = []
    for number, (place, count) in enumerate([(ix, gx), (iy, gy), (iz, gz)]):
        for end in range(2):
            device = [ix, iy, iz]
            device[number] = place + (-1 if end == 0 else 1)
            inner = place > 0 if end == 0 else place < count - 1
            near_ones.append((number, end, inner, tuple(device)))

    outside = jnp.where(lax.rem(lane, 4) < 2, 1.25, 0.0).astype(F32)
    for number, end, inner, device in near_ones:

        @pl.when(jnp.logical_not(inner))
        def _(number=number, end=end):
            for level in range(STEPS):
                if number == 0:
                    x = 0 if end == 0 else bx + 1
                    state[level, 0, x, middle, :] = jnp.full((by, bz), 1.25, F32)
                    state[level, 1, x, middle, :] = jnp.zeros((by, bz), F32)
                elif number == 1:
                    shape = (GROUPS, 1, SLOTS, bz)
                    hy_got[level, end, :, pl.ds(0, 1)] = jnp.full(shape, 1.25, F32)
                    hy_got[level, end, :, pl.ds(1, 1)] = jnp.zeros(shape, F32)
                else:
                    hz_got[level, end] = jnp.broadcast_to(outside, (GROUPS, by, 128))

    def offer(level, g):
        packed = jnp.zeros((by, 128), F32)
        for slot in range(SLOTS):
            x = spot(g, slot) + 1
            heat = state[level, 0, x, middle, :]
            cond = state[level, 1, x, middle, :]
            for f, values in ((0, heat), (1, cond)):
                hy_send[level, 0, g, f, pl.ds(slot, 1), :] = values[:1]
                hy_send[level, 1, g, f, pl.ds(slot, 1), :] = values[by - 1 :]
            ends = jnp.where(lane < 2, pltpu.roll(heat, 1, 1), pltpu.roll(cond, 3, 1))
            if slot:
                ends = pltpu.roll(ends, 4 * slot, 1)
            packed = jnp.where(lane // 4 == slot, ends, packed)
        hz_send[level, g] = packed
        for number, end, inner, device in near_ones:
            if number == 0:
                continue

            @pl.when(inner)
            def _(number=number, end=end, device=device):
                src = hy_send.at[level, end, g] if number == 1 else hz_send.at[level, g]
                dst = (hy_got if number == 1 else hz_got).at[level, 1 - end, g]
                remote(
                    src,
                    dst,
                    hs_sem.at[level, number - 1, end, g],
                    hr_sem.at[level, number - 1, 1 - end, g],
                    device,
                )

    def offer_ends(level):
        for number, end, inner, device in near_ones[:2]:

            @pl.when(inner)
            def _(end=end, device=device):
                remote(
                    state.at[level, :, 1 if end == 0 else bx, middle, :],
                    state.at[level, :, bx + 1 if end == 0 else 0, middle, :],
                    hxs_sem.at[level, end],
                    hxr_sem.at[level, 1 - end],
                    device,
                )

    def accept_ends(level):
        for number, end, inner, device in near_ones[:2]:

            @pl.when(inner)
            def _(end=end):
                settle(
                    state.at[level, :, 0 if end == 0 else bx + 1, middle, :],
                    hxr_sem.at[level, end],
                )

    def accept(level, g):
        for number, end, inner, device in near_ones[2:]:

            @pl.when(inner)
            def _(number=number, end=end):
                settle(
                    (hy_got if number == 1 else hz_got).at[level, end, g],
                    hr_sem.at[level, number - 1, end, g],
                )

        for slot in range(SLOTS):
            x = spot(g, slot) + 1
            for f in range(2):
                row = pl.ds(slot, 1)
                state[level, f, x, pl.ds(7, 1), :] = hy_got[level, 0, g, f, row, :]
                state[level, f, x, pl.ds(8 + by, 1), :] = hy_got[level, 1, g, f, row, :]

    pieces = [pl.ds(k * PIECE, PIECE) for k in range(by // PIECE)]

    def flux_of(level, g, slot, piece):
        x = spot(g, slot) + 1

        def at(f, dx, dy):
            return state[level, f, x + dx, pl.ds(8 + piece.start + dy, PIECE), :]

        heat, cond = at(0, 0, 0), at(1, 0, 0)
        around = [(at(0, dx, dy), at(1, dx, dy)) for dx, dy in ((1, 0), (-1, 0), (0, 1), (0, -1))]
        for end in range(2):
            packed = hz_got[level, end, g, piece, :]
            edge = 0 if end == 0 else 127
            turn = 1 if end == 0 else 127
            pair = []
            for f, values in ((0, heat), (1, cond)):
                shift = (edge - (4 * slot + 2 * f + end)) % 128
                beyond = pltpu.roll(packed, shift, 1) if shift else packed
                pair.append(jnp.where(lane == edge, beyond, pltpu.roll(values, turn, 1)))
            around.append(tuple(pair))
        flux = None
        for heat_side, cond_side in around:
            term = (cond + cond_side) * (heat_side - heat)
            flux = term if flux is None else flux + term
        return x, heat, flux

    def prepare(g, carry):
        accept(0, g)
        for slot in range(SLOTS):
            for piece in pieces:
                x, heat, flux = flux_of(0, g, slot, piece)
                state[1, 0, x, pl.ds(8 + piece.start, PIECE), :] = heat + 0.08 * flux
                inverse[x - 1, piece, :] = -1.0 / heat
        return carry

    def first_step(g, carry):
        for slot in range(SLOTS):
            x = spot(g, slot)
            rho = rho_v[x]
            growth = jnp.exp(thr[x] * inverse[x]) * (1.0 - rho)
            state[1, 0, x + 1, middle, :] = state[1, 0, x + 1, middle, :] + 0.48 * growth
            rho = rho + 0.64 * growth
            rho_v[x] = rho
            state[1, 1, x + 1, middle, :] = rho * rho
        offer(1, g)

        @pl.when(g == 0)
        def _():
            offer_ends(1)

        return carry

    def later_step(level):
        def group(g, carry):
            @pl.when(g == 0)
            def _():
                accept_ends(level)

            accept(level, g)
            for slot in range(SLOTS):
                for piece in pieces:
                    x, heat, flux = flux_of(level, g, slot, piece)
                    rho = rho_v[x - 1, piece, :]
                    growth = jnp.exp(-thr[x - 1, piece, :] / heat) * (1.0 - rho)
                    heat = heat + (0.08 * flux + 0.48 * growth)
                    rho = rho + 0.64 * growth
                    rho_v[x - 1, piece, :] = rho
                    if level + 1 < STEPS:
                        rows = pl.ds(8 + piece.start, PIECE)
                        state[level + 1, 0, x, rows, :] = heat
                        state[level + 1, 1, x, rows, :] = rho * rho
                    else:
                        heat_last[x - 1, piece, :] = heat
            if level + 1 < STEPS:
                offer(level + 1, g)

                @pl.when(g == 0)
                def _():
                    offer_ends(level + 1)

            return carry

        lax.fori_loop(0, GROUPS, group, 0)

    def conduct(x, carry):
        rho = rho_v[x]
        state[0, 1, x + 1, middle, :] = rho * rho
        return carry

    def offer_first(g, carry):
        offer(0, g)
        return carry

    def locate():
        x = sensors[0:1, :] - ix * bx
        y = sensors[1:2, :] - iy * by
        z = sensors[2:3, :] - iz * bz
        own = (x >= 0) & (x < bx) & (y >= 0) & (y < by) & (z >= 0) & (z < bz)
        code = jnp.where(own, (x * by + y) * bz + z, -1)
        cells = [code[:, t * 128 : t * 128 + 128] for t in range(S // 128)]
        last_one = functools.reduce(
            jnp.maximum, [jnp.where(c >= 0, c + t * (bx * by * bz), -1) for t, c in enumerate(cells)]
        )
        count = functools.reduce(jnp.add, [jnp.where(c >= 0, 1, 0) for c in cells])
        code_out[...] = jnp.concatenate([code, last_one, count], axis=1)

    stage1(0)
    met()

    def pipeline(i, carry):
        @pl.when((i > 0) & (i < CHUNKS))
        def _():
            stage1(i)

        @pl.when(i < CHUNKS)
        def _():
            ship1(i)

        @pl.when(i == 0)
        def _():
            loads[3].wait()
            loads[4].wait()
            lax.fori_loop(0, bx, conduct, 0)
            offer_ends(0)
            lax.fori_loop(0, GROUPS, offer_first, 0)
            loads[5].wait()
            loads[6].wait()

        @pl.when((i >= 1) & (i <= CHUNKS))
        def _():
            stage2(i - 1)

        @pl.when(i == 2)
        def _():
            locate()
            accept_ends(0)

        @pl.when((i >= 2) & (i < 2 + GROUPS))
        def _():
            prepare(i - 2, 0)

        @pl.when(i >= LAG)
        def _():
            stage3(i - LAG)

        return carry

    lax.fori_loop(0, CHUNKS + LAG, pipeline, 0)

    settle(got3, r3_sem.at[0])
    for x in range(half):
        turned = got3[pl.ds(x, bz, stride=half), :].T
        thr[x] = turned[:by]
        thr[half + x] = turned[by:]
    thr_copy = pltpu.make_async_copy(thr, thr_out, out_sem.at[0])
    thr_copy.start()

    lax.fori_loop(0, GROUPS, first_step, 0)
    for level in range(1, STEPS):
        later_step(level)
    heat_copy = pltpu.make_async_copy(heat_last, heat_out, out_sem.at[1])
    rho_copy = pltpu.make_async_copy(rho_v, rho_out, out_sem.at[2])
    heat_copy.start()
    rho_copy.start()

    def drain_chunk(c, carry):
        settle(send1.at[c, pl.ds(0, (nd - 1) * part)], s1_sem.at[c])
        settle(send2.at[c, pl.ds(0, gx - 1)], s2_sem.at[c])
        return carry

    lax.fori_loop(0, CHUNKS, drain_chunk, 0)
    settle(send3.at[:, pl.ds(0, gy - 1)], s3_sem.at[0])
    for number, end, inner, device in near_ones:

        @pl.when(inner)
        def _(number=number, end=end):
            for level in range(STEPS):
                if number == 0:
                    settle(
                        state.at[level, :, 1 if end == 0 else bx, middle, :],
                        hxs_sem.at[level, end],
                    )
                    continue
                for g in range(GROUPS):
                    settle(
                        hy_send.at[level, end, g] if number == 1 else hz_send.at[level, g],
                        hs_sem.at[level, number - 1, end, g],
                    )

    thr_copy.wait()
    heat_copy.wait()
    rho_copy.wait()


def read_kernel(
    by, code_hbm, thr, rho, heat, thr_out, rho_out, heat_out, found, code, thr_v, rho_v, heat_v, sem
):
    codes = pltpu.make_async_copy(code_hbm, code, sem.at[6])
    ins = [
        pltpu.make_async_copy(src, dst, sem.at[k])
        for k, (src, dst) in enumerate(((heat, heat_v), (thr, thr_v), (rho, rho_v)))
    ]
    outs = [
        pltpu.make_async_copy(src, dst, sem.at[3 + k])
        for k, (src, dst) in enumerate(((heat_v, heat_out), (thr_v, thr_out), (rho_v, rho_out)))
    ]
    codes.start()
    for copy in ins:
        copy.start()
    found[...] = jnp.zeros(found.shape, F32)
    lane = lax.broadcasted_iota(jnp.int32, (1, 128), 1)
    for copy, after in zip(ins, outs):
        copy.wait()
        after.start()
    codes.wait()

    block = heat_v.shape[0] * by * 128

    def read(t, j):
        cell = jnp.bitwise_and(code[0, t * 128 + j], block - 1)
        place = jnp.right_shift(cell, 7)
        row = heat_v[place // by, pl.ds(lax.rem(place, by), 1), :]
        turned = pltpu.roll(row, jnp.bitwise_and(j - cell, 127), 1)
        target = pl.ds(t, 1)
        found[target, :] = jnp.where(lane == j, turned, found[target, :])

    def quad(q, carry):
        lasts = [code[0, S + 4 * q + t] for t in range(4)]

        @pl.when(functools.reduce(jnp.maximum, lasts) >= 0)
        def _():
            def column(j, carry):
                final = code[0, S + j]

                @pl.when(final >= 0)
                def _():
                    number = jnp.right_shift(final, block.bit_length() - 1)
                    alone = code[0, S + 128 + j] == 1

                    def one(t, carry):
                        @pl.when(code[0, t * 128 + j] >= 0)
                        def _():
                            read(t, j)

                        return carry

                    lax.fori_loop(jnp.where(alone, number, 0), number + 1, one, 0)

                return carry

            lax.fori_loop(4 * q, 4 * q + 4, column, 0)

        return carry

    lax.fori_loop(0, 32, quad, 0)
    for copy in outs:
        copy.wait()


def sum_kernel(
    dims, cost, found, recorded, model_out, odds_out, red_a, mid_b, red_b, mid_c, red_c, mid_d,
    red_d, rs_sem, rr_sem,
):
    gx, gy, gz = dims
    (ix, iy, iz), _, line_device, row_device = places(gx, gy, gz)
    per = S // 128 // gz
    lines = [line_device(k) for k in LINE_ORDER]
    rows = [row_device(offset) for offset in ROW_ORDER]
    quads = [lax.rem(iz + k, gz) for k in (2, 1, 3)]
    quads = [(other, (ix, iy, other)) for other in quads]
    barrier = pltpu.get_barrier_semaphore()
    partners = lines + rows + quads
    for _, device in partners:
        pl.semaphore_signal(barrier, inc=1, device_id=device, device_id_type=MESH)

    def piece(k):
        return pl.ds(pl.multiple_of(k * per, per), per)

    red_a[iz] = found[piece(iz), :]
    pl.semaphore_wait(barrier, len(partners))
    for other, device in quads:
        remote(found.at[piece(other), :], red_a.at[iz], rs_sem.at[0], rr_sem.at[0], device)
    settle(red_a.at[pl.ds(0, gz - 1)], rr_sem.at[0])
    mid_b[...] = jnp.sum(red_a[...], axis=0)
    for other, device in lines:
        remote(mid_b, red_b.at[ix], rs_sem.at[1], rr_sem.at[1], device)
    red_b[ix] = mid_b[...]
    settle(red_b.at[pl.ds(0, gx - 1)], rr_sem.at[1])
    mid_c[...] = jnp.sum(red_b[...], axis=0)
    for other, device in rows:
        remote(mid_c, red_c.at[iy], rs_sem.at[2], rr_sem.at[2], device)
    red_c[iy] = mid_c[...]
    settle(red_c.at[pl.ds(0, gy - 1)], rr_sem.at[2])
    mid_d[...] = jnp.sum(red_c[...], axis=0)
    for other, device in quads:
        remote(mid_d, red_d.at[iz], rs_sem.at[3], rr_sem.at[3], device)
    red_d[iz] = mid_d[...]
    settle(red_d.at[pl.ds(0, gz - 1)], rr_sem.at[3])
    values = red_d[...].reshape(S // 128, 128)
    model_out[...] = values
    gap = (values - recorded[...]) / 0.2
    odds_out[0] = cost[0] - 0.5 * (jnp.sum(gap * gap) / S)
    settle(red_a.at[pl.ds(0, gz - 1)], rs_sem.at[0])
    settle(red_b.at[pl.ds(0, gx - 1)], rs_sem.at[1])
    settle(red_c.at[pl.ds(0, gy - 1)], rs_sem.at[2])
    settle(red_d.at[pl.ds(0, gz - 1)], rs_sem.at[3])


def solution(mesh):
    gx, gy, gz = (mesh.shape[name] for name in ("gx", "gy", "gz"))
    nx, ny, nz = MESH_EXTENT_EAST, MESH_EXTENT_NORTH, MESH_EXTENT_UPWARD
    depth, first, second = tables(gx, gy, gz, nx, ny, nz)
    nd = gy * gz
    sub = nz // nd
    part = sub // CHUNKS
    bx, by, bz = nx // gx, ny // gy, nz // gz
    kx_own, ky_own = nx // nd, ny // gx
    per = S // 128 // gz
    smem = pl.BlockSpec(memory_space=pltpu.SMEM)
    hbm = pl.BlockSpec(memory_space=pl.ANY)
    vmem = pl.BlockSpec(memory_space=pltpu.VMEM)
    dma = pltpu.SemaphoreType.DMA
    block = jax.ShapeDtypeStruct((bx, by, bz), F32)

    def body(incumbent, renewed, beta, rho, heat, place, recorded, cost):
        energy, density, kelvin, code = pl.pallas_call(
            functools.partial(kernel, (gx, gy, gz, nx, ny, nz)),
            out_shape=(
                block,
                block,
                block,
                jax.ShapeDtypeStruct((1, S + 256), jnp.int32),
            ),
            in_specs=[smem] + [hbm] * 7 + [vmem],
            out_specs=(hbm, hbm, hbm, vmem),
            scratch_shapes=[
                pltpu.VMEM((2, kx_own, ky_own, nz), F32),
                pltpu.VMEM((2, kx_own, ky_own, nz), F32),
                pltpu.VMEM((kx_own * 2 * ky_own, nz), BF16),
                pltpu.VMEM((kx_own * 2 * ky_own, nz), BF16),
                pltpu.VMEM(depth.shape, BF16),
                pltpu.VMEM(first.shape, BF16),
                pltpu.VMEM(second.shape, BF16),
                pltpu.VMEM((CHUNKS, nd * part, kx_own, 128), F32),
                pltpu.VMEM((CHUNKS, nd, part, kx_own, 128), F32),
                pltpu.VMEM((CHUNKS, gx, part, bx, 128), F32),
                pltpu.VMEM((CHUNKS, gx, part, bx, 128), F32),
                pltpu.VMEM((CHUNKS, gy, part * bx // 2, 128), F32),
                pltpu.VMEM((bz * bx // 2, 128), F32),
                pltpu.VMEM((bx, by, bz), F32),
                pltpu.VMEM((bx, by, bz), F32),
                pltpu.VMEM((STEPS, 2, bx + 2, by + 16, bz), F32),
                pltpu.VMEM((bx, by, bz), F32),
                pltpu.VMEM((bx, by, bz), F32),
                pltpu.VMEM((STEPS, 2, GROUPS, 2, SLOTS, bz), F32),
                pltpu.VMEM((STEPS, 2, GROUPS, 2, SLOTS, bz), F32),
                pltpu.VMEM((STEPS, GROUPS, by, bz), F32),
                pltpu.VMEM((STEPS, 2, GROUPS, by, bz), F32),
                dma((7,)),
                dma((3,)),
                dma((CHUNKS,)),
                dma((CHUNKS,)),
                dma((CHUNKS,)),
                dma((CHUNKS,)),
                dma((1,)),
                dma((1,)),
                dma((STEPS, 2)),
                dma((STEPS, 2)),
                dma((STEPS, 2, 2, GROUPS)),
                dma((STEPS, 2, 2, GROUPS)),
            ],
            compiler_params=pltpu.CompilerParams(
                collective_id=0, has_side_effects=True, vmem_limit_bytes=56 * 1024 * 1024
            ),
            cost_estimate=pl.CostEstimate(
                flops=7_000_000_000, bytes_accessed=16_000_000, transcendentals=1_000_000
            ),
        )(
            beta,
            incumbent,
            renewed,
            jnp.asarray(depth),
            jnp.asarray(first),
            jnp.asarray(second),
            rho,
            heat,
            place.T,
        )
        energy, density, kelvin, found = pl.pallas_call(
            functools.partial(read_kernel, by),
            out_shape=(block, block, block, jax.ShapeDtypeStruct((S // 128, 128), F32)),
            in_specs=[hbm] * 4,
            out_specs=(hbm, hbm, hbm, vmem),
            scratch_shapes=[pltpu.SMEM((1, S + 256), jnp.int32)]
            + [pltpu.VMEM((bx, by, bz), F32)] * 3
            + [dma((7,))],
            compiler_params=pltpu.CompilerParams(vmem_limit_bytes=60 * 1024 * 1024),
        )(code, energy, density, kelvin)
        model, odds = pl.pallas_call(
            functools.partial(sum_kernel, (gx, gy, gz)),
            out_shape=(
                jax.ShapeDtypeStruct((S // 128, 128), F32),
                jax.ShapeDtypeStruct((1,), F32),
            ),
            in_specs=[smem, vmem, vmem],
            out_specs=(vmem, smem),
            scratch_shapes=[
                pltpu.VMEM((gz, per, 128), F32),
                pltpu.VMEM((per, 128), F32),
                pltpu.VMEM((gx, per, 128), F32),
                pltpu.VMEM((per, 128), F32),
                pltpu.VMEM((gy, per, 128), F32),
                pltpu.VMEM((per, 128), F32),
                pltpu.VMEM((gz, per, 128), F32),
                dma((4,)),
                dma((4,)),
            ],
            compiler_params=pltpu.CompilerParams(collective_id=1, has_side_effects=True),
        )(cost, found, recorded.reshape(S // 128, 128))
        return energy, density, kelvin, model.reshape(S), odds

    return jax.shard_map(
        body,
        mesh=mesh,
        in_specs=(
            P(None, ("gy", "gz"), "gx", None),
            P(None, ("gy", "gz"), "gx", None),
            P(),
            P("gx", "gy", "gz"),
            P("gx", "gy", "gz"),
            P(),
            P(),
            P(),
        ),
        out_specs=(P("gx", "gy", "gz"), P("gx", "gy", "gz"), P("gx", "gy", "gz"), P(), P()),
        check_vma=False,
    )
```

```python
import functools
import math

import jax
import jax.numpy as jnp
import ml_dtypes
import numpy as np
from jax import lax
from jax.experimental import pallas as pl
from jax.experimental.pallas import tpu as pltpu
from jax.sharding import PartitionSpec as P

MESH_EXTENT_EAST = 256
MESH_EXTENT_NORTH = 512
MESH_EXTENT_UPWARD = 512
STEPS = 3
S = 4096
CHUNKS = 8
LAG = 3
GROUPS = 4
SLOTS = 8
PIECE = 16
ABL = set()
MESH = pl.DeviceIdType.MESH
F32 = jnp.float32
BF16 = jnp.bfloat16
NT = (((1,), (1,)), ((), ()))


def spectrum(length):
    wave = np.arange(length)
    signed = np.where(wave < length // 2, wave, wave - length).astype(np.float64)
    shape = 1.0 / np.sqrt(1.0 + (signed / 8.0) ** 2)
    return shape / np.sqrt(np.sum(shape * shape))


def waves(places, numbers, length):
    angle = (places[:, None] * numbers[None, :] % length) * (2.0 * math.pi / length)
    scale = spectrum(length)[numbers][None, :]
    return np.cos(angle) * scale, np.sin(angle) * scale


def halves(table):
    high = table.astype(np.float32).astype(ml_dtypes.bfloat16)
    low = (table - high.astype(np.float64)).astype(np.float32).astype(ml_dtypes.bfloat16)
    return high, low


def tables(gx, gy, gz, nx, ny, nz):
    sub = nz // (gy * gz)
    part = sub // CHUNKS
    stacks = []
    for chunk in range(CHUNKS):
        places = np.concatenate(
            [
                z * (nz // gz) + y * sub + chunk * part + np.arange(part)
                for y in range(gy)
                for z in range(gz)
            ]
        )
        cosine, sine = waves(places, np.arange(nz), nz)
        stacks.append(np.concatenate(halves(np.concatenate([cosine, sine]))))
    depth = np.stack(stacks)
    cosine, sine = waves(np.arange(nx), np.arange(nx), nx)
    first = np.concatenate(halves(np.concatenate([cosine, sine])))
    width = ny // gx
    blocks = []
    for block in range(gx):
        cosine, sine = waves(np.arange(ny), block * width + np.arange(width), ny)
        blocks += [cosine.T, -sine.T]
    second = np.stack(halves(np.concatenate(blocks)))
    return depth, first, second


def split(values):
    high = values.astype(BF16)
    return high, (values - high.astype(F32)).astype(BF16)


PLANE_ORDER = [
    (dx, dy, dc)
    for dx, dy in [
        (2, 2), (1, 0), (0, 1), (3, 0), (0, 3), (2, 1), (1, 2), (2, 3),
        (3, 2), (1, 1), (3, 3), (2, 0), (0, 2), (1, 3), (3, 1), (0, 0),
    ]
    for dc in range(2)
    if (dx, dy, dc) != (0, 0, 0)
]
LINE_ORDER = [4, 3, -3, 2, -2, 1, -1]
ROW_ORDER = [(2, 1), (1, 0), (3, 1), (2, 0), (1, 1), (3, 0), (0, 1)]


def places(gx, gy, gz):
    ix, iy, iz = lax.axis_index("gx"), lax.axis_index("gy"), lax.axis_index("gz")
    nx_ring = gy // 2
    x, y_high = lax.rem(iy, nx_ring), iy // nx_ring
    y, core = y_high * (gz // 2) + iz // 2, lax.rem(iz, 2)
    turn = 1 - 2 * core

    def plane(offset):
        dx, dy, dc = offset
        to_x = lax.rem(x + turn * dx + 2 * nx_ring, nx_ring)
        to_y = lax.rem(y + turn * dy + 2 * gz, gz)
        to_core = lax.rem(core + dc, 2)
        to = ((to_y // 2) * nx_ring + to_x, lax.rem(to_y, 2) * 2 + to_core)
        return to[0] * gz + to[1], (ix,) + to

    def line(k):
        other = lax.rem(ix + turn * k + 2 * gx, gx)
        return other, (other, iy, iz)

    def row(offset):
        dx, dy = offset
        other = lax.rem(y_high + dy, 2) * nx_ring + lax.rem(x + turn * dx + 2 * nx_ring, nx_ring)
        return other, (ix, other, iz)

    return (ix, iy, iz), plane, line, row


def greet(plane, line):
    barrier = pltpu.get_barrier_semaphore()
    for offset in PLANE_ORDER:
        pl.semaphore_signal(barrier, inc=1, device_id=plane(offset)[1], device_id_type=MESH)
    for offset in LINE_ORDER:
        pl.semaphore_signal(barrier, inc=1, device_id=line(offset)[1], device_id_type=MESH)


def met():
    pl.semaphore_wait(pltpu.get_barrier_semaphore(), len(PLANE_ORDER) + len(LINE_ORDER))


def remote(src, dst, send_sem, recv_sem, device):
    pltpu.make_async_remote_copy(
        src_ref=src,
        dst_ref=dst,
        send_sem=send_sem,
        recv_sem=recv_sem,
        device_id=device,
        device_id_type=MESH,
    ).start()


def settle(ref, sem):
    pltpu.make_async_copy(ref, ref, sem).wait()


def kernel(
    dims,
    beta,
    inc,
    ren,
    w1_hbm,
    w2_hbm,
    w3_hbm,
    rho0,
    heat0,
    sensors_hbm,
    thr_out,
    rho_out,
    heat_out,
    code_out,
    sensors,
    inc_v,
    ren_v,
    b_high,
    b_low,
    w1,
    w2,
    w3,
    send1,
    got1,
    send2,
    got2,
    send3,
    got3,
    thr,
    inverse,
    state,
    heat_last,
    rho_v,
    hy_send,
    hy_got,
    hz_send,
    hz_got,
    load_sem,
    out_sem,
    s1_sem,
    r1_sem,
    s2_sem,
    r2_sem,
    s3_sem,
    r3_sem,
    hxs_sem,
    hxr_sem,
    hs_sem,
    hr_sem,
):
    gx, gy, gz, nx, ny, nz = dims
    nd = gy * gz
    sub = nz // nd
    part = sub // CHUNKS
    bx, by, bz = nx // gx, ny // gy, nz // gz
    half = bx // 2
    kx_own = nx // nd
    (ix, iy, iz), plane_device, line_device, row_device = places(gx, gy, gz)
    me = iy * gz + iz
    middle = pl.ds(8, by)

    greet(plane_device, line_device)
    loads = [
        pltpu.make_async_copy(inc, inc_v, load_sem.at[0]),
        pltpu.make_async_copy(ren, ren_v, load_sem.at[1]),
        pltpu.make_async_copy(w1_hbm, w1, load_sem.at[2]),
        pltpu.make_async_copy(heat0, state.at[0, 0, pl.ds(1, bx), middle, :], load_sem.at[3]),
        pltpu.make_async_copy(rho0, rho_v, load_sem.at[4]),
        pltpu.make_async_copy(w2_hbm, w2, load_sem.at[5]),
        pltpu.make_async_copy(w3_hbm, w3, load_sem.at[6]),
        pltpu.make_async_copy(sensors_hbm, sensors, load_sem.at[7]),
    ]
    for load in loads:
        load.start()
    lane = lax.broadcasted_iota(jnp.int32, (1, 128), 1)
    sign = jnp.where(lane < 64, -1.0, 1.0).astype(F32)
    first_half = lane < 64

    loads[0].wait()
    loads[1].wait()
    weight = jnp.full((1, 128), beta[0], F32)
    keep = jnp.sqrt(1.0 - weight * weight)[:, :1]
    fresh = weight[:, :1]

    def mix(k, carry):
        for part_of in range(2):
            mixed = keep * inc_v[part_of, k] + fresh * ren_v[part_of, k]
            high, low = split(mixed)
            rows = pl.ds(pl.multiple_of(k * 128 + part_of * 64, 64), 64)
            b_high[rows, :] = high
            b_low[rows, :] = low
        return carry

    lax.fori_loop(0, kx_own, mix, 0)
    loads[2].wait()

    rows1 = nd * part

    def stage1(c):
        flat = send1.at[c].reshape(rows1 * kx_own, 128)
        for q in range(kx_own // 2):
            right = pl.ds(q * 256, 256)
            top = lax.dot_general(w1[c], b_high[right, :], NT, preferred_element_type=F32)
            low = lax.dot_general(
                w1[c, pl.ds(0, 2 * rows1), :], b_low[right, :], NT, preferred_element_type=F32
            )
            total = top[: 2 * rows1] + top[2 * rows1 :] + low
            for side in range(2):
                cut = slice(side * 128, side * 128 + 128)
                cosines = total[:rows1, cut]
                sines = total[rows1:, cut]
                flat[pl.ds(2 * q + side, rows1, stride=kx_own), :] = cosines + sign * pltpu.roll(
                    sines, 64, 1
                )

    def ship1(c):
        for offset in PLANE_ORDER:
            other, device = plane_device(offset)
            remote(
                send1.at[c, pl.ds(other * part, part)],
                got1.at[c, me],
                s1_sem.at[c],
                r1_sem.at[c],
                device,
            )
        pltpu.make_async_copy(
            send1.at[c, pl.ds(me * part, part)], got1.at[c, me], r1_sem.at[c]
        ).start()

    def stage2(c):
        settle(got1.at[c], r1_sem.at[c])
        for p in range(part // 2):
            values = jnp.concatenate(
                [got1[c, :, 2 * p + side].reshape(nx, 128) for side in range(2)], axis=1
            )
            high, low = split(values)
            top = jnp.dot(w2[...], high, preferred_element_type=F32)
            bottom = jnp.dot(w2[pl.ds(0, 2 * nx), :], low, preferred_element_type=F32)
            total = top[: 2 * nx] + top[2 * nx :] + bottom
            for side in range(2):
                cut = slice(side * 128, side * 128 + 128)
                result = total[:nx, cut] + sign * pltpu.roll(total[nx:, cut], 64, 1)
                send2[c, :, 2 * p + side] = result.reshape(gx, bx, 128)
        for k in LINE_ORDER:
            other, device = line_device(k)
            remote(send2.at[c, other], got2.at[c, ix], s2_sem.at[c], r2_sem.at[c], device)
        pltpu.make_async_copy(send2.at[c, ix], got2.at[c, ix], r2_sem.at[c]).start()

    def stage3(c):
        settle(got2.at[c], r2_sem.at[c])
        rows = part * bx
        values = jnp.concatenate([got2[c, g].reshape(rows, 128) for g in range(gx)], axis=1)
        high, low = split(values)
        both = jnp.concatenate([high, low], axis=0)
        for t in range(ny // 256):
            columns = pl.ds(t * 256, 256)
            top = jnp.dot(both, w3[0, :, columns], preferred_element_type=F32)
            field = (
                top[:rows]
                + top[rows:]
                + jnp.dot(high, w3[1, :, columns], preferred_element_type=F32)
            )
            energy = 2.0 + 0.6 * jnp.tanh(field)
            for side in range(2):
                tile = energy[:, side * 128 : side * 128 + 128].reshape(part, 2, half, 128)
                near = tile[:, 0].reshape(part * half, 128)
                far = tile[:, 1].reshape(part * half, 128)
                j = 4 * t + 2 * side
                send3[c, j] = jnp.where(first_half, near, pltpu.roll(far, 64, 1))
                send3[c, j + 1] = jnp.where(first_half, pltpu.roll(near, 64, 1), far)
        target = got3.at[
            pl.ds(pl.multiple_of((iy * sub + c * part) * half, part * half), part * half), :
        ]
        for offset in ROW_ORDER:
            other, device = row_device(offset)
            remote(send3.at[c, other], target, s3_sem.at[0], r3_sem.at[0], device)
        pltpu.make_async_copy(send3.at[c, iy], target, r3_sem.at[0]).start()

    def spot(g, slot):
        return lax.rem(g * (SLOTS // 2) + slot // 2 + half - 1, half) + slot % 2 * half

    near_ones = []
    for number, (place, count) in enumerate([(ix, gx), (iy, gy), (iz, gz)]):
        for end in range(2):
            device = [ix, iy, iz]
            device[number] = place + (-1 if end == 0 else 1)
            inner = place > 0 if end == 0 else place < count - 1
            near_ones.append((number, end, inner, tuple(device)))

    outside = jnp.where(lax.rem(lane, 4) < 2, 1.25, 0.0).astype(F32)
    for number, end, inner, device in near_ones:

        @pl.when(jnp.logical_not(inner))
        def _(number=number, end=end):
            for level in range(STEPS):
                if number == 0:
                    x = 0 if end == 0 else bx + 1
                    state[level, 0, x, middle, :] = jnp.full((by, bz), 1.25, F32)
                    state[level, 1, x, middle, :] = jnp.zeros((by, bz), F32)
                elif number == 1:
                    shape = (GROUPS, 1, SLOTS, bz)
                    hy_got[level, end, :, pl.ds(0, 1)] = jnp.full(shape, 1.25, F32)
                    hy_got[level, end, :, pl.ds(1, 1)] = jnp.zeros(shape, F32)
                else:
                    hz_got[level, end] = jnp.broadcast_to(outside, (GROUPS, by, 128))

    def offer(level, g):
        packed = jnp.zeros((by, 128), F32)
        for slot in range(SLOTS):
            x = spot(g, slot) + 1
            heat = state[level, 0, x, middle, :]
            cond = state[level, 1, x, middle, :]
            for f, values in ((0, heat), (1, cond)):
                hy_send[level, 0, g, f, pl.ds(slot, 1), :] = values[:1]
                hy_send[level, 1, g, f, pl.ds(slot, 1), :] = values[by - 1 :]
            ends = jnp.where(lane < 2, pltpu.roll(heat, 1, 1), pltpu.roll(cond, 3, 1))
            if slot:
                ends = pltpu.roll(ends, 4 * slot, 1)
            packed = jnp.where(lane // 4 == slot, ends, packed)
        hz_send[level, g] = packed
        for number, end, inner, device in near_ones:
            if number == 0:
                continue

            @pl.when(inner)
            def _(number=number, end=end, device=device):
                src = hy_send.at[level, end, g] if number == 1 else hz_send.at[level, g]
                dst = (hy_got if number == 1 else hz_got).at[level, 1 - end, g]
                remote(
                    src,
                    dst,
                    hs_sem.at[level, number - 1, end, g],
                    hr_sem.at[level, number - 1, 1 - end, g],
                    device,
                )

    def offer_ends(level):
        for number, end, inner, device in near_ones[:2]:

            @pl.when(inner)
            def _(end=end, device=device):
                remote(
                    state.at[level, :, 1 if end == 0 else bx, middle, :],
                    state.at[level, :, bx + 1 if end == 0 else 0, middle, :],
                    hxs_sem.at[level, end],
                    hxr_sem.at[level, 1 - end],
                    device,
                )

    def accept_ends(level):
        for number, end, inner, device in near_ones[:2]:

            @pl.when(inner)
            def _(end=end):
                settle(
                    state.at[level, :, 0 if end == 0 else bx + 1, middle, :],
                    hxr_sem.at[level, end],
                )

    def accept(level, g):
        for number, end, inner, device in near_ones[2:]:

            @pl.when(inner)
            def _(number=number, end=end):
                settle(
                    (hy_got if number == 1 else hz_got).at[level, end, g],
                    hr_sem.at[level, number - 1, end, g],
                )

        for slot in range(SLOTS):
            x = spot(g, slot) + 1
            for f in range(2):
                row = pl.ds(slot, 1)
                state[level, f, x, pl.ds(7, 1), :] = hy_got[level, 0, g, f, row, :]
                state[level, f, x, pl.ds(8 + by, 1), :] = hy_got[level, 1, g, f, row, :]

    pieces = [pl.ds(k * PIECE, PIECE) for k in range(by // PIECE)]

    def flux_of(level, g, slot, piece):
        x = spot(g, slot) + 1

        def at(f, dx, dy):
            return state[level, f, x + dx, pl.ds(8 + piece.start + dy, PIECE), :]

        heat, cond = at(0, 0, 0), at(1, 0, 0)
        around = [(at(0, dx, dy), at(1, dx, dy)) for dx, dy in ((1, 0), (-1, 0), (0, 1), (0, -1))]
        for end in range(2):
            packed = hz_got[level, end, g, piece, :]
            edge = 0 if end == 0 else 127
            turn = 1 if end == 0 else 127
            pair = []
            for f, values in ((0, heat), (1, cond)):
                shift = (edge - (4 * slot + 2 * f + end)) % 128
                beyond = pltpu.roll(packed, shift, 1) if shift else packed
                pair.append(jnp.where(lane == edge, beyond, pltpu.roll(values, turn, 1)))
            around.append(tuple(pair))
        flux = None
        for heat_side, cond_side in around:
            term = (cond + cond_side) * (heat_side - heat)
            flux = term if flux is None else flux + term
        return x, heat, flux

    def prepare(g, carry):
        accept(0, g)
        for slot in range(SLOTS):
            for piece in pieces:
                x, heat, flux = flux_of(0, g, slot, piece)
                state[1, 0, x, pl.ds(8 + piece.start, PIECE), :] = heat + 0.08 * flux
                inverse[x - 1, piece, :] = -1.0 / heat
        return carry

    def first_step(g, carry):
        for slot in range(0, SLOTS, 2):
            x = spot(g, slot)
            turned = got3[pl.ds(x, bz, stride=half), :].T
            thr[x] = turned[:by]
            thr[half + x] = turned[by:]
        for slot in range(SLOTS):
            x = spot(g, slot)
            rho = rho_v[x]
            growth = jnp.exp(thr[x] * inverse[x]) * (1.0 - rho)
            state[1, 0, x + 1, middle, :] = state[1, 0, x + 1, middle, :] + 0.48 * growth
            rho = rho + 0.64 * growth
            rho_v[x] = rho
            state[1, 1, x + 1, middle, :] = rho * rho

        @pl.when(g == 0)
        def _():
            offer_ends(1)

        offer(1, g)
        return carry

    def grow(level):
        def plane(x, carry):
            rho = rho_v[x]
            growth = jnp.exp(-thr[x] / state[level, 0, x + 1, middle, :]) * (1.0 - rho)
            inverse[x] = 0.48 * growth
            rho = rho + 0.64 * growth
            rho_v[x] = rho
            if level + 1 < STEPS:
                state[level + 1, 1, x + 1, middle, :] = rho * rho
            return carry

        lax.fori_loop(0, bx, plane, 0, unroll=4)

    def later_step(level):
        def group(g, carry):
            @pl.when(g == 0)
            def _():
                accept_ends(level)

            accept(level, g)
            for slot in range(SLOTS):
                for piece in pieces:
                    x, heat, flux = flux_of(level, g, slot, piece)
                    heat = heat + (0.08 * flux + inverse[x - 1, piece, :])
                    if level + 1 < STEPS:
                        state[level + 1, 0, x, pl.ds(8 + piece.start, PIECE), :] = heat
                    else:
                        heat_last[x - 1, piece, :] = heat
            if level + 1 < STEPS:

                @pl.when(g == 0)
                def _():
                    offer_ends(level + 1)

                offer(level + 1, g)

            return carry

        lax.fori_loop(0, GROUPS, group, 0)

    def conduct(x, carry):
        rho = rho_v[x]
        state[0, 1, x + 1, middle, :] = rho * rho
        return carry

    def offer_first(g, carry):
        offer(0, g)
        return carry

    def locate():
        loads[7].wait()
        x = sensors[0:1, :] - ix * bx
        y = sensors[1:2, :] - iy * by
        z = sensors[2:3, :] - iz * bz
        own = (x >= 0) & (x < bx) & (y >= 0) & (y < by) & (z >= 0) & (z < bz)
        code = jnp.where(own, (x * by + y) * bz + z, -1)
        cells = [code[:, t * 128 : t * 128 + 128] for t in range(S // 128)]
        last_one = functools.reduce(
            jnp.maximum, [jnp.where(c >= 0, c + t * (bx * by * bz), -1) for t, c in enumerate(cells)]
        )
        count = functools.reduce(jnp.add, [jnp.where(c >= 0, 1, 0) for c in cells])
        code_out[...] = jnp.concatenate([code, last_one, count], axis=1)

    stage1(0)
    met()

    def pipeline(i, carry):
        @pl.when((i > 0) & (i < CHUNKS))
        def _():
            stage1(i)

        @pl.when(i < CHUNKS)
        def _():
            ship1(i)

        @pl.when(i == 0)
        def _():
            loads[3].wait()
            loads[4].wait()
            lax.fori_loop(0, bx, conduct, 0)
            offer_ends(0)
            lax.fori_loop(0, GROUPS, offer_first, 0)
            loads[5].wait()
            loads[6].wait()

        @pl.when((i >= 1) & (i <= CHUNKS))
        def _():
            stage2(i - 1)

        @pl.when(i == 2)
        def _():
            locate()
            accept_ends(0)

        @pl.when((i >= 2) & (i < 2 + GROUPS))
        def _():
            prepare(i - 2, 0)

        @pl.when(i >= LAG)
        def _():
            stage3(i - LAG)

        return carry

    lax.fori_loop(0, CHUNKS + LAG, pipeline, 0)

    settle(got3, r3_sem.at[0])
    lax.fori_loop(0, GROUPS, first_step, 0)
    thr_copy = pltpu.make_async_copy(thr, thr_out, out_sem.at[0])
    thr_copy.start()
    rho_copy = pltpu.make_async_copy(rho_v, rho_out, out_sem.at[2])
    for level in range(1, STEPS):
        grow(level)
        if level + 1 == STEPS:
            rho_copy.start()
        later_step(level)
    heat_copy = pltpu.make_async_copy(heat_last, heat_out, out_sem.at[1])
    heat_copy.start()

    def drain_chunk(c, carry):
        settle(send1.at[c, pl.ds(0, (nd - 1) * part)], s1_sem.at[c])
        settle(send2.at[c, pl.ds(0, gx - 1)], s2_sem.at[c])
        return carry

    lax.fori_loop(0, CHUNKS, drain_chunk, 0)
    settle(send3.at[:, pl.ds(0, gy - 1)], s3_sem.at[0])
    for number, end, inner, device in near_ones:

        @pl.when(inner)
        def _(number=number, end=end):
            for level in range(STEPS):
                if number == 0:
                    settle(
                        state.at[level, :, 1 if end == 0 else bx, middle, :],
                        hxs_sem.at[level, end],
                    )
                    continue
                for g in range(GROUPS):
                    settle(
                        hy_send.at[level, end, g] if number == 1 else hz_send.at[level, g],
                        hs_sem.at[level, number - 1, end, g],
                    )

    thr_copy.wait()
    heat_copy.wait()
    rho_copy.wait()


def read_kernel(
    by, code_hbm, thr, rho, heat, thr_out, rho_out, heat_out, found, code, thr_v, rho_v, heat_v, sem
):
    codes = pltpu.make_async_copy(code_hbm, code, sem.at[6])
    ins = [
        pltpu.make_async_copy(src, dst, sem.at[k])
        for k, (src, dst) in enumerate(((heat, heat_v), (thr, thr_v), (rho, rho_v)))
    ]
    outs = [
        pltpu.make_async_copy(src, dst, sem.at[3 + k])
        for k, (src, dst) in enumerate(((heat_v, heat_out), (thr_v, thr_out), (rho_v, rho_out)))
    ]
    codes.start()
    ins[0].start()
    lane = lax.broadcasted_iota(jnp.int32, (1, 128), 1)
    ins[0].wait()
    outs[0].start()
    for copy in ins[1:]:
        copy.start()
    codes.wait()

    block = heat_v.shape[0] * by * 128

    row_of = lax.broadcasted_iota(jnp.int32, (found.shape[0], 128), 0)

    def fetch(cell, j):
        place = jnp.right_shift(cell, 7)
        row = heat_v[jnp.right_shift(place, by.bit_length() - 1), pl.ds(place & (by - 1), 1), :]
        return pltpu.roll(row, (j - cell) & 127, 1)

    def columns(q, total):
        for k in range(16):
            j = 16 * q + k
            final = code[0, S + j]
            value = fetch(final & (block - 1), j)
            number = jnp.right_shift(final, block.bit_length() - 1)
            total = jnp.where((row_of == number) & (lane == j), value, total)
        return total

    found[...] = lax.fori_loop(0, 8, columns, jnp.zeros(found.shape, F32))

    for copy, after in zip(ins[1:], outs[1:]):
        copy.wait()
        after.start()

    def quad(q, carry):
        counts = [code[0, S + 128 + 4 * q + t] for t in range(4)]

        @pl.when(functools.reduce(jnp.maximum, counts) > 1)
        def _():
            def column(j, carry):
                @pl.when(code[0, S + 128 + j] > 1)
                def _():
                    def one(t, carry):
                        cell = code[0, t * 128 + j]

                        @pl.when(cell >= 0)
                        def _():
                            target = pl.ds(t, 1)
                            found[target, :] = jnp.where(lane == j, fetch(cell, j), found[target, :])

                        return carry

                    lax.fori_loop(0, jnp.right_shift(code[0, S + j], block.bit_length() - 1), one, 0)

                return carry

            lax.fori_loop(4 * q, 4 * q + 4, column, 0)

        return carry

    lax.fori_loop(0, 32, quad, 0)
    for copy in outs:
        copy.wait()


def sum_kernel(
    dims, cost, found_hbm, recorded_hbm, model_out, odds_out, found, recorded, red_a, mid_b, red_b, mid_c, red_c, mid_d,
    red_d, load_sem, rs_sem, rr_sem,
):
    gx, gy, gz = dims
    (ix, iy, iz), _, line_device, row_device = places(gx, gy, gz)
    per = S // 128 // gz
    lines = [line_device(k) for k in LINE_ORDER]
    rows = [row_device(offset) for offset in ROW_ORDER]
    quads = [lax.rem(iz + k, gz) for k in (2, 1, 3)]
    quads = [(other, (ix, iy, other)) for other in quads]
    barrier = pltpu.get_barrier_semaphore()
    partners = lines + rows + quads
    for _, device in partners:
        pl.semaphore_signal(barrier, inc=1, device_id=device, device_id_type=MESH)

    def piece(k):
        return pl.ds(pl.multiple_of(k * per, per), per)

    loads = [
        pltpu.make_async_copy(found_hbm, found, load_sem.at[0]),
        pltpu.make_async_copy(recorded_hbm, recorded, load_sem.at[1]),
    ]
    for load in loads:
        load.start()
    loads[0].wait()
    red_a[iz] = found[piece(iz), :]
    pl.semaphore_wait(barrier, len(partners))
    for other, device in quads:
        remote(found.at[piece(other), :], red_a.at[iz], rs_sem.at[0], rr_sem.at[0], device)
    settle(red_a.at[pl.ds(0, gz - 1)], rr_sem.at[0])
    mid_b[...] = jnp.sum(red_a[...], axis=0)
    for other, device in lines:
        remote(mid_b, red_b.at[ix], rs_sem.at[1], rr_sem.at[1], device)
    red_b[ix] = mid_b[...]
    settle(red_b.at[pl.ds(0, gx - 1)], rr_sem.at[1])
    mid_c[...] = jnp.sum(red_b[...], axis=0)
    for other, device in rows:
        remote(mid_c, red_c.at[iy], rs_sem.at[2], rr_sem.at[2], device)
    red_c[iy] = mid_c[...]
    settle(red_c.at[pl.ds(0, gy - 1)], rr_sem.at[2])
    mid_d[...] = jnp.sum(red_c[...], axis=0)
    for other, device in quads:
        remote(mid_d, red_d.at[iz], rs_sem.at[3], rr_sem.at[3], device)
    red_d[iz] = mid_d[...]
    settle(red_d.at[pl.ds(0, gz - 1)], rr_sem.at[3])
    loads[1].wait()
    values = red_d[...].reshape(S // 128, 128)
    model_out[...] = values
    gap = (values - recorded[...]) / 0.2
    odds_out[0] = cost[0] - 0.5 * (jnp.sum(gap * gap) / S)
    settle(red_a.at[pl.ds(0, gz - 1)], rs_sem.at[0])
    settle(red_b.at[pl.ds(0, gx - 1)], rs_sem.at[1])
    settle(red_c.at[pl.ds(0, gy - 1)], rs_sem.at[2])
    settle(red_d.at[pl.ds(0, gz - 1)], rs_sem.at[3])


def solution(mesh):
    gx, gy, gz = (mesh.shape[name] for name in ("gx", "gy", "gz"))
    nx, ny, nz = MESH_EXTENT_EAST, MESH_EXTENT_NORTH, MESH_EXTENT_UPWARD
    depth, first, second = tables(gx, gy, gz, nx, ny, nz)
    nd = gy * gz
    sub = nz // nd
    part = sub // CHUNKS
    bx, by, bz = nx // gx, ny // gy, nz // gz
    kx_own, ky_own = nx // nd, ny // gx
    per = S // 128 // gz
    smem = pl.BlockSpec(memory_space=pltpu.SMEM)
    hbm = pl.BlockSpec(memory_space=pl.ANY)
    vmem = pl.BlockSpec(memory_space=pltpu.VMEM)
    dma = pltpu.SemaphoreType.DMA
    block = jax.ShapeDtypeStruct((bx, by, bz), F32)

    def body(incumbent, renewed, beta, rho, heat, place, recorded, cost):
        energy, density, kelvin, code = pl.pallas_call(
            functools.partial(kernel, (gx, gy, gz, nx, ny, nz)),
            out_shape=(
                block,
                block,
                block,
                jax.ShapeDtypeStruct((1, S + 256), jnp.int32),
            ),
            in_specs=[smem] + [hbm] * 8,
            out_specs=(hbm, hbm, hbm, vmem),
            scratch_shapes=[
                pltpu.VMEM((3, S), jnp.int32),
                pltpu.VMEM((2, kx_own, ky_own, nz), F32),
                pltpu.VMEM((2, kx_own, ky_own, nz), F32),
                pltpu.VMEM((kx_own * 2 * ky_own, nz), BF16),
                pltpu.VMEM((kx_own * 2 * ky_own, nz), BF16),
                pltpu.VMEM(depth.shape, BF16),
                pltpu.VMEM(first.shape, BF16),
                pltpu.VMEM(second.shape, BF16),
                pltpu.VMEM((CHUNKS, nd * part, kx_own, 128), F32),
                pltpu.VMEM((CHUNKS, nd, part, kx_own, 128), F32),
                pltpu.VMEM((CHUNKS, gx, part, bx, 128), F32),
                pltpu.VMEM((CHUNKS, gx, part, bx, 128), F32),
                pltpu.VMEM((CHUNKS, gy, part * bx // 2, 128), F32),
                pltpu.VMEM((bz * bx // 2, 128), F32),
                pltpu.VMEM((bx, by, bz), F32),
                pltpu.VMEM((bx, by, bz), F32),
                pltpu.VMEM((STEPS, 2, bx + 2, by + 16, bz), F32),
                pltpu.VMEM((bx, by, bz), F32),
                pltpu.VMEM((bx, by, bz), F32),
                pltpu.VMEM((STEPS, 2, GROUPS, 2, SLOTS, bz), F32),
                pltpu.VMEM((STEPS, 2, GROUPS, 2, SLOTS, bz), F32),
                pltpu.VMEM((STEPS, GROUPS, by, bz), F32),
                pltpu.VMEM((STEPS, 2, GROUPS, by, bz), F32),
                dma((8,)),
                dma((3,)),
                dma((CHUNKS,)),
                dma((CHUNKS,)),
                dma((CHUNKS,)),
                dma((CHUNKS,)),
                dma((1,)),
                dma((1,)),
                dma((STEPS, 2)),
                dma((STEPS, 2)),
                dma((STEPS, 2, 2, GROUPS)),
                dma((STEPS, 2, 2, GROUPS)),
            ],
            compiler_params=pltpu.CompilerParams(
                collective_id=0, has_side_effects=True, vmem_limit_bytes=56 * 1024 * 1024
            ),
            cost_estimate=pl.CostEstimate(
                flops=7_000_000_000, bytes_accessed=16_000_000, transcendentals=1_000_000
            ),
        )(
            beta,
            incumbent,
            renewed,
            jnp.asarray(depth),
            jnp.asarray(first),
            jnp.asarray(second),
            rho,
            heat,
            place.T,
        )
        energy, density, kelvin, found = pl.pallas_call(
            functools.partial(read_kernel, by),
            out_shape=(block, block, block, jax.ShapeDtypeStruct((S // 128, 128), F32)),
            in_specs=[hbm] * 4,
            out_specs=(hbm, hbm, hbm, vmem),
            scratch_shapes=[pltpu.SMEM((1, S + 256), jnp.int32)]
            + [pltpu.VMEM((bx, by, bz), F32)] * 3
            + [dma((7,))],
            compiler_params=pltpu.CompilerParams(vmem_limit_bytes=60 * 1024 * 1024),
        )(code, energy, density, kelvin)
        model, odds = pl.pallas_call(
            functools.partial(sum_kernel, (gx, gy, gz)),
            out_shape=(
                jax.ShapeDtypeStruct((S // 128, 128), F32),
                jax.ShapeDtypeStruct((1,), F32),
            ),
            in_specs=[smem, hbm, hbm],
            out_specs=(vmem, smem),
            scratch_shapes=[
                pltpu.VMEM((S // 128, 128), F32),
                pltpu.VMEM((S // 128, 128), F32),
                pltpu.VMEM((gz, per, 128), F32),
                pltpu.VMEM((per, 128), F32),
                pltpu.VMEM((gx, per, 128), F32),
                pltpu.VMEM((per, 128), F32),
                pltpu.VMEM((gy, per, 128), F32),
                pltpu.VMEM((per, 128), F32),
                pltpu.VMEM((gz, per, 128), F32),
                dma((2,)),
                dma((4,)),
                dma((4,)),
            ],
            compiler_params=pltpu.CompilerParams(
                collective_id=1, has_side_effects=True, vmem_limit_bytes=60 * 1024 * 1024
            ),
        )(cost, found, recorded.reshape(S // 128, 128))
        return energy, density, kelvin, model.reshape(S), odds

    return jax.shard_map(
        body,
        mesh=mesh,
        in_specs=(
            P(None, ("gy", "gz"), "gx", None),
            P(None, ("gy", "gz"), "gx", None),
            P(),
            P("gx", "gy", "gz"),
            P("gx", "gy", "gz"),
            P(),
            P(),
            P(),
        ),
        out_specs=(P("gx", "gy", "gz"), P("gx", "gy", "gz"), P("gx", "gy", "gz"), P(), P()),
        check_vma=False,
    )
```

```python
import functools
import math

import jax
import jax.numpy as jnp
import ml_dtypes
import numpy as np
from jax import lax
from jax.experimental import pallas as pl
from jax.experimental.pallas import tpu as pltpu
from jax.sharding import PartitionSpec as P

MESH_EXTENT_EAST = 256
MESH_EXTENT_NORTH = 512
MESH_EXTENT_UPWARD = 512
STEPS = 3
S = 4096
CHUNKS = 8
LAG = 3
GROUPS = 4
SLOTS = 8
PIECE = 16
ABL = set()
MESH = pl.DeviceIdType.MESH
F32 = jnp.float32
BF16 = jnp.bfloat16
NT = (((1,), (1,)), ((), ()))


def spectrum(length):
    wave = np.arange(length)
    signed = np.where(wave < length // 2, wave, wave - length).astype(np.float64)
    shape = 1.0 / np.sqrt(1.0 + (signed / 8.0) ** 2)
    return shape / np.sqrt(np.sum(shape * shape))


def waves(places, numbers, length):
    angle = (places[:, None] * numbers[None, :] % length) * (2.0 * math.pi / length)
    scale = spectrum(length)[numbers][None, :]
    return np.cos(angle) * scale, np.sin(angle) * scale


def halves(table):
    high = table.astype(np.float32).astype(ml_dtypes.bfloat16)
    low = (table - high.astype(np.float64)).astype(np.float32).astype(ml_dtypes.bfloat16)
    return high, low


def tables(gx, gy, gz, nx, ny, nz):
    sub = nz // (gy * gz)
    part = sub // CHUNKS
    stacks = []
    for chunk in range(CHUNKS):
        places = np.concatenate(
            [
                z * (nz // gz) + y * sub + chunk * part + np.arange(part)
                for y in range(gy)
                for z in range(gz)
            ]
        )
        cosine, sine = waves(places, np.arange(nz), nz)
        stacks.append(np.concatenate(halves(np.concatenate([cosine, sine]))))
    depth = np.stack(stacks)
    cosine, sine = waves(np.arange(nx), np.arange(nx), nx)
    first = np.concatenate(halves(np.concatenate([cosine, sine])))
    width = ny // gx
    blocks = []
    for block in range(gx):
        cosine, sine = waves(np.arange(ny), block * width + np.arange(width), ny)
        blocks += [cosine.T, -sine.T]
    second = np.stack(halves(np.concatenate(blocks)))
    return depth, first, second


def split(values):
    high = values.astype(BF16)
    return high, (values - high.astype(F32)).astype(BF16)


PLANE_ORDER = [
    (dx, dy, dc)
    for dx, dy in [
        (2, 2), (1, 0), (0, 1), (3, 0), (0, 3), (2, 1), (1, 2), (2, 3),
        (3, 2), (1, 1), (3, 3), (2, 0), (0, 2), (1, 3), (3, 1), (0, 0),
    ]
    for dc in range(2)
    if (dx, dy, dc) != (0, 0, 0)
]
LINE_ORDER = [4, 3, -3, 2, -2, 1, -1]
FAR_FIRST = sorted(PLANE_ORDER, key=lambda o: -min(o[0], 4 - o[0]) - min(o[1], 4 - o[1]))
ROW_ORDER = [(2, 1), (1, 0), (3, 1), (2, 0), (1, 1), (3, 0), (0, 1)]


def places(gx, gy, gz):
    ix, iy, iz = lax.axis_index("gx"), lax.axis_index("gy"), lax.axis_index("gz")
    nx_ring = gy // 2
    x, y_high = lax.rem(iy, nx_ring), iy // nx_ring
    y, core = y_high * (gz // 2) + iz // 2, lax.rem(iz, 2)
    turn = 1 - 2 * core

    def plane(offset):
        dx, dy, dc = offset
        to_x = lax.rem(x + turn * dx + 2 * nx_ring, nx_ring)
        to_y = lax.rem(y + turn * dy + 2 * gz, gz)
        to_core = lax.rem(core + dc, 2)
        to = ((to_y // 2) * nx_ring + to_x, lax.rem(to_y, 2) * 2 + to_core)
        return to[0] * gz + to[1], (ix,) + to

    def line(k):
        other = lax.rem(ix + turn * k + 2 * gx, gx)
        return other, (other, iy, iz)

    def row(offset):
        dx, dy = offset
        other = lax.rem(y_high + dy, 2) * nx_ring + lax.rem(x + turn * dx + 2 * nx_ring, nx_ring)
        return other, (ix, other, iz)

    return (ix, iy, iz), plane, line, row


def greet(plane, line):
    barrier = pltpu.get_barrier_semaphore()
    devices = [line(k)[1] for k in LINE_ORDER[:3]]
    devices += [plane(offset)[1] for offset in FAR_FIRST]
    devices += [line(k)[1] for k in LINE_ORDER[3:]]
    for device in devices:
        pl.semaphore_signal(barrier, inc=1, device_id=device, device_id_type=MESH)


def met():
    pl.semaphore_wait(pltpu.get_barrier_semaphore(), len(PLANE_ORDER) + len(LINE_ORDER))


def remote(src, dst, send_sem, recv_sem, device):
    pltpu.make_async_remote_copy(
        src_ref=src,
        dst_ref=dst,
        send_sem=send_sem,
        recv_sem=recv_sem,
        device_id=device,
        device_id_type=MESH,
    ).start()


def settle(ref, sem):
    pltpu.make_async_copy(ref, ref, sem).wait()


def kernel(
    dims,
    beta,
    inc,
    ren,
    w1_hbm,
    w2_hbm,
    w3_hbm,
    rho0,
    heat0,
    sensors_hbm,
    thr_out,
    rho_out,
    heat_out,
    code_out,
    sensors,
    inc_v,
    ren_v,
    b_high,
    b_low,
    w1,
    w2,
    w3,
    send1,
    got1,
    send2,
    got2,
    send3,
    got3,
    thr,
    inverse,
    state,
    heat_last,
    rho_v,
    hy_send,
    hy_got,
    hz_send,
    hz_got,
    load_sem,
    out_sem,
    s1_sem,
    r1_sem,
    s2_sem,
    r2_sem,
    s3_sem,
    r3_sem,
    hxs_sem,
    hxr_sem,
    hs_sem,
    hr_sem,
):
    gx, gy, gz, nx, ny, nz = dims
    nd = gy * gz
    sub = nz // nd
    part = sub // CHUNKS
    bx, by, bz = nx // gx, ny // gy, nz // gz
    half = bx // 2
    kx_own = nx // nd
    (ix, iy, iz), plane_device, line_device, row_device = places(gx, gy, gz)
    me = iy * gz + iz
    middle = pl.ds(8, by)

    greet(plane_device, line_device)
    loads = [
        pltpu.make_async_copy(inc, inc_v, load_sem.at[0]),
        pltpu.make_async_copy(ren, ren_v, load_sem.at[1]),
        pltpu.make_async_copy(w1_hbm, w1, load_sem.at[2]),
        pltpu.make_async_copy(heat0, state.at[0, 0, pl.ds(1, bx), middle, :], load_sem.at[3]),
        pltpu.make_async_copy(rho0, rho_v, load_sem.at[4]),
        pltpu.make_async_copy(w2_hbm, w2, load_sem.at[5]),
        pltpu.make_async_copy(w3_hbm, w3, load_sem.at[6]),
        pltpu.make_async_copy(sensors_hbm, sensors, load_sem.at[7]),
    ]
    for load in loads:
        load.start()
    lane = lax.broadcasted_iota(jnp.int32, (1, 128), 1)
    sign = jnp.where(lane < 64, -1.0, 1.0).astype(F32)
    first_half = lane < 64

    loads[0].wait()
    loads[1].wait()
    weight = jnp.full((1, 128), beta[0], F32)
    keep = jnp.sqrt(1.0 - weight * weight)[:, :1]
    fresh = weight[:, :1]

    def mix(k, carry):
        for part_of in range(2):
            mixed = keep * inc_v[part_of, k] + fresh * ren_v[part_of, k]
            high, low = split(mixed)
            rows = pl.ds(pl.multiple_of(k * 128 + part_of * 64, 64), 64)
            b_high[rows, :] = high
            b_low[rows, :] = low
        return carry

    lax.fori_loop(0, kx_own, mix, 0)
    loads[2].wait()

    rows1 = nd * part

    def stage1(c):
        flat = send1.at[c].reshape(rows1 * kx_own, 128)
        for q in range(kx_own // 2):
            right = pl.ds(q * 256, 256)
            top = lax.dot_general(w1[c], b_high[right, :], NT, preferred_element_type=F32)
            low = lax.dot_general(
                w1[c, pl.ds(0, 2 * rows1), :], b_low[right, :], NT, preferred_element_type=F32
            )
            total = top[: 2 * rows1] + top[2 * rows1 :] + low
            for side in range(2):
                cut = slice(side * 128, side * 128 + 128)
                cosines = total[:rows1, cut]
                sines = total[rows1:, cut]
                flat[pl.ds(2 * q + side, rows1, stride=kx_own), :] = cosines + sign * pltpu.roll(
                    sines, 64, 1
                )

    def ship1(c):
        for offset in FAR_FIRST:
            other, device = plane_device(offset)
            remote(
                send1.at[c, pl.ds(other * part, part)],
                got1.at[c, me],
                s1_sem.at[c],
                r1_sem.at[c],
                device,
            )
        pltpu.make_async_copy(
            send1.at[c, pl.ds(me * part, part)], got1.at[c, me], r1_sem.at[c]
        ).start()

    def stage2(c):
        settle(got1.at[c], r1_sem.at[c])
        for p in range(part // 2):
            values = jnp.concatenate(
                [got1[c, :, 2 * p + side].reshape(nx, 128) for side in range(2)], axis=1
            )
            high, low = split(values)
            top = jnp.dot(w2[...], high, preferred_element_type=F32)
            bottom = jnp.dot(w2[pl.ds(0, 2 * nx), :], low, preferred_element_type=F32)
            total = top[: 2 * nx] + top[2 * nx :] + bottom
            for side in range(2):
                cut = slice(side * 128, side * 128 + 128)
                result = total[:nx, cut] + sign * pltpu.roll(total[nx:, cut], 64, 1)
                send2[c, :, 2 * p + side] = result.reshape(gx, bx, 128)
        for k in LINE_ORDER:
            other, device = line_device(k)
            remote(send2.at[c, other], got2.at[c, ix], s2_sem.at[c], r2_sem.at[c], device)
        pltpu.make_async_copy(send2.at[c, ix], got2.at[c, ix], r2_sem.at[c]).start()

    def stage3(c):
        settle(got2.at[c], r2_sem.at[c])
        rows = part * bx
        values = jnp.concatenate([got2[c, g].reshape(rows, 128) for g in range(gx)], axis=1)
        high, low = split(values)
        both = jnp.concatenate([high, low], axis=0)
        for t in range(ny // 256):
            columns = pl.ds(t * 256, 256)
            top = jnp.dot(both, w3[0, :, columns], preferred_element_type=F32)
            field = (
                top[:rows]
                + top[rows:]
                + jnp.dot(high, w3[1, :, columns], preferred_element_type=F32)
            )
            energy = 2.0 + 0.6 * jnp.tanh(field)
            for side in range(2):
                tile = energy[:, side * 128 : side * 128 + 128].reshape(part, 2, half, 128)
                near = tile[:, 0].reshape(part * half, 128)
                far = tile[:, 1].reshape(part * half, 128)
                j = 4 * t + 2 * side
                send3[c, j] = jnp.where(first_half, near, pltpu.roll(far, 64, 1))
                send3[c, j + 1] = jnp.where(first_half, pltpu.roll(near, 64, 1), far)
        target = got3.at[
            pl.ds(pl.multiple_of((iy * sub + c * part) * half, part * half), part * half), :
        ]
        for offset in ROW_ORDER:
            other, device = row_device(offset)
            remote(send3.at[c, other], target, s3_sem.at[0], r3_sem.at[0], device)
        pltpu.make_async_copy(send3.at[c, iy], target, r3_sem.at[0]).start()

    def spot(g, slot):
        return lax.rem(g * (SLOTS // 2) + slot // 2 + half - 1, half) + slot % 2 * half

    near_ones = []
    for number, (place, count) in enumerate([(ix, gx), (iy, gy), (iz, gz)]):
        for end in range(2):
            device = [ix, iy, iz]
            device[number] = place + (-1 if end == 0 else 1)
            inner = place > 0 if end == 0 else place < count - 1
            near_ones.append((number, end, inner, tuple(device)))

    outside = jnp.where(lax.rem(lane, 4) < 2, 1.25, 0.0).astype(F32)
    for number, end, inner, device in near_ones:

        @pl.when(jnp.logical_not(inner))
        def _(number=number, end=end):
            for level in range(STEPS):
                if number == 0:
                    x = 0 if end == 0 else bx + 1
                    state[level, 0, x, middle, :] = jnp.full((by, bz), 1.25, F32)
                    state[level, 1, x, middle, :] = jnp.zeros((by, bz), F32)
                elif number == 1:
                    shape = (GROUPS, 1, SLOTS, bz)
                    hy_got[level, end, :, pl.ds(0, 1)] = jnp.full(shape, 1.25, F32)
                    hy_got[level, end, :, pl.ds(1, 1)] = jnp.zeros(shape, F32)
                else:
                    hz_got[level, end] = jnp.broadcast_to(outside, (GROUPS, by, 128))

    def offer(level, g):
        packed = jnp.zeros((by, 128), F32)
        for slot in range(SLOTS):
            x = spot(g, slot) + 1
            heat = state[level, 0, x, middle, :]
            cond = state[level, 1, x, middle, :]
            for f, values in ((0, heat), (1, cond)):
                hy_send[level, 0, g, f, pl.ds(slot, 1), :] = values[:1]
                hy_send[level, 1, g, f, pl.ds(slot, 1), :] = values[by - 1 :]
            ends = jnp.where(lane < 2, pltpu.roll(heat, 1, 1), pltpu.roll(cond, 3, 1))
            if slot:
                ends = pltpu.roll(ends, 4 * slot, 1)
            packed = jnp.where(lane // 4 == slot, ends, packed)
        hz_send[level, g] = packed
        for number, end, inner, device in near_ones:
            if number == 0:
                continue

            @pl.when(inner)
            def _(number=number, end=end, device=device):
                src = hy_send.at[level, end, g] if number == 1 else hz_send.at[level, g]
                dst = (hy_got if number == 1 else hz_got).at[level, 1 - end, g]
                remote(
                    src,
                    dst,
                    hs_sem.at[level, number - 1, end, g],
                    hr_sem.at[level, number - 1, 1 - end, g],
                    device,
                )

    def offer_ends(level):
        for number, end, inner, device in near_ones[:2]:

            @pl.when(inner)
            def _(end=end, device=device):
                remote(
                    state.at[level, :, 1 if end == 0 else bx, middle, :],
                    state.at[level, :, bx + 1 if end == 0 else 0, middle, :],
                    hxs_sem.at[level, end],
                    hxr_sem.at[level, 1 - end],
                    device,
                )

    def accept_ends(level):
        for number, end, inner, device in near_ones[:2]:

            @pl.when(inner)
            def _(end=end):
                settle(
                    state.at[level, :, 0 if end == 0 else bx + 1, middle, :],
                    hxr_sem.at[level, end],
                )

    def accept(level, g):
        for number, end, inner, device in near_ones[2:]:

            @pl.when(inner)
            def _(number=number, end=end):
                settle(
                    (hy_got if number == 1 else hz_got).at[level, end, g],
                    hr_sem.at[level, number - 1, end, g],
                )

        for slot in range(SLOTS):
            x = spot(g, slot) + 1
            for f in range(2):
                row = pl.ds(slot, 1)
                state[level, f, x, pl.ds(7, 1), :] = hy_got[level, 0, g, f, row, :]
                state[level, f, x, pl.ds(8 + by, 1), :] = hy_got[level, 1, g, f, row, :]

    pieces = [pl.ds(k * PIECE, PIECE) for k in range(by // PIECE)]

    def flux_of(level, g, slot, piece):
        x = spot(g, slot) + 1

        def at(f, dx, dy):
            return state[level, f, x + dx, pl.ds(8 + piece.start + dy, PIECE), :]

        heat, cond = at(0, 0, 0), at(1, 0, 0)
        around = [(at(0, dx, dy), at(1, dx, dy)) for dx, dy in ((1, 0), (-1, 0), (0, 1), (0, -1))]
        for end in range(2):
            packed = hz_got[level, end, g, piece, :]
            edge = 0 if end == 0 else 127
            turn = 1 if end == 0 else 127
            pair = []
            for f, values in ((0, heat), (1, cond)):
                shift = (edge - (4 * slot + 2 * f + end)) % 128
                beyond = pltpu.roll(packed, shift, 1) if shift else packed
                pair.append(jnp.where(lane == edge, beyond, pltpu.roll(values, turn, 1)))
            around.append(tuple(pair))
        flux = None
        for heat_side, cond_side in around:
            term = (cond + cond_side) * (heat_side - heat)
            flux = term if flux is None else flux + term
        return x, heat, flux

    def prepare(g, carry):
        accept(0, g)
        for slot in range(SLOTS):
            for piece in pieces:
                x, heat, flux = flux_of(0, g, slot, piece)
                state[1, 0, x, pl.ds(8 + piece.start, PIECE), :] = heat + 0.08 * flux
                inverse[x - 1, piece, :] = -1.0 / heat
        return carry

    def first_step(g, carry):
        for slot in range(0, SLOTS, 2):
            x = spot(g, slot)
            turned = got3[pl.ds(x, bz, stride=half), :].T
            thr[x] = turned[:by]
            thr[half + x] = turned[by:]
        for slot in range(SLOTS):
            x = spot(g, slot)
            rho = rho_v[x]
            growth = jnp.exp(thr[x] * inverse[x]) * (1.0 - rho)
            state[1, 0, x + 1, middle, :] = state[1, 0, x + 1, middle, :] + 0.48 * growth
            rho = rho + 0.64 * growth
            rho_v[x] = rho
            state[1, 1, x + 1, middle, :] = rho * rho

        @pl.when(g == 0)
        def _():
            offer_ends(1)

        offer(1, g)
        return carry

    def grow(level):
        def plane(x, carry):
            rho = rho_v[x]
            growth = jnp.exp(-thr[x] / state[level, 0, x + 1, middle, :]) * (1.0 - rho)
            inverse[x] = 0.48 * growth
            rho = rho + 0.64 * growth
            rho_v[x] = rho
            if level + 1 < STEPS:
                state[level + 1, 1, x + 1, middle, :] = rho * rho
            return carry

        lax.fori_loop(0, bx, plane, 0, unroll=4)

    def later_step(level):
        def group(g, carry):
            @pl.when(g == 0)
            def _():
                accept_ends(level)

            accept(level, g)
            for slot in range(SLOTS):
                for piece in pieces:
                    x, heat, flux = flux_of(level, g, slot, piece)
                    heat = heat + (0.08 * flux + inverse[x - 1, piece, :])
                    if level + 1 < STEPS:
                        state[level + 1, 0, x, pl.ds(8 + piece.start, PIECE), :] = heat
                    else:
                        heat_last[x - 1, piece, :] = heat
            if level + 1 < STEPS:

                @pl.when(g == 0)
                def _():
                    offer_ends(level + 1)

                offer(level + 1, g)

            return carry

        lax.fori_loop(0, GROUPS, group, 0)

    def conduct(x, carry):
        rho = rho_v[x]
        state[0, 1, x + 1, middle, :] = rho * rho
        return carry

    def offer_first(g, carry):
        offer(0, g)
        return carry

    def locate():
        loads[7].wait()
        x = sensors[0:1, :] - ix * bx
        y = sensors[1:2, :] - iy * by
        z = sensors[2:3, :] - iz * bz
        own = (x >= 0) & (x < bx) & (y >= 0) & (y < by) & (z >= 0) & (z < bz)
        code = jnp.where(own, (x * by + y) * bz + z, -1)
        cells = [code[:, t * 128 : t * 128 + 128] for t in range(S // 128)]
        last_one = functools.reduce(
            jnp.maximum, [jnp.where(c >= 0, c + t * (bx * by * bz), -1) for t, c in enumerate(cells)]
        )
        count = functools.reduce(jnp.add, [jnp.where(c >= 0, 1, 0) for c in cells])
        code_out[...] = jnp.concatenate([code, last_one, count], axis=1)

    stage1(0)
    met()

    def pipeline(i, carry):
        @pl.when((i > 0) & (i < CHUNKS))
        def _():
            stage1(i)

        @pl.when(i < CHUNKS)
        def _():
            ship1(i)

        @pl.when(i == 0)
        def _():
            loads[3].wait()
            loads[4].wait()
            lax.fori_loop(0, bx, conduct, 0)
            offer_ends(0)
            lax.fori_loop(0, GROUPS, offer_first, 0)
            loads[5].wait()
            loads[6].wait()

        @pl.when((i >= 1) & (i <= CHUNKS))
        def _():
            stage2(i - 1)

        @pl.when(i == 2)
        def _():
            locate()
            accept_ends(0)

        @pl.when((i >= 2) & (i < 2 + GROUPS))
        def _():
            prepare(i - 2, 0)

        @pl.when(i >= LAG)
        def _():
            stage3(i - LAG)

        return carry

    lax.fori_loop(0, CHUNKS + LAG, pipeline, 0)

    settle(got3, r3_sem.at[0])
    lax.fori_loop(0, GROUPS, first_step, 0)
    thr_copy = pltpu.make_async_copy(thr, thr_out, out_sem.at[0])
    thr_copy.start()
    rho_copy = pltpu.make_async_copy(rho_v, rho_out, out_sem.at[2])
    for level in range(1, STEPS):
        grow(level)
        if level + 1 == STEPS:
            rho_copy.start()
        later_step(level)
    heat_copy = pltpu.make_async_copy(heat_last, heat_out, out_sem.at[1])
    heat_copy.start()

    def drain_chunk(c, carry):
        settle(send1.at[c, pl.ds(0, (nd - 1) * part)], s1_sem.at[c])
        settle(send2.at[c, pl.ds(0, gx - 1)], s2_sem.at[c])
        return carry

    lax.fori_loop(0, CHUNKS, drain_chunk, 0)
    settle(send3.at[:, pl.ds(0, gy - 1)], s3_sem.at[0])
    for number, end, inner, device in near_ones:

        @pl.when(inner)
        def _(number=number, end=end):
            for level in range(STEPS):
                if number == 0:
                    settle(
                        state.at[level, :, 1 if end == 0 else bx, middle, :],
                        hxs_sem.at[level, end],
                    )
                    continue
                for g in range(GROUPS):
                    settle(
                        hy_send.at[level, end, g] if number == 1 else hz_send.at[level, g],
                        hs_sem.at[level, number - 1, end, g],
                    )

    thr_copy.wait()
    heat_copy.wait()
    rho_copy.wait()


def read_kernel(
    by, code_hbm, thr, rho, heat, thr_out, rho_out, heat_out, found, code, thr_v, rho_v, heat_v, sem
):
    codes = pltpu.make_async_copy(code_hbm, code, sem.at[6])
    ins = [
        pltpu.make_async_copy(src, dst, sem.at[k])
        for k, (src, dst) in enumerate(((heat, heat_v), (thr, thr_v), (rho, rho_v)))
    ]
    outs = [
        pltpu.make_async_copy(src, dst, sem.at[3 + k])
        for k, (src, dst) in enumerate(((heat_v, heat_out), (thr_v, thr_out), (rho_v, rho_out)))
    ]
    codes.start()
    ins[0].start()
    lane = lax.broadcasted_iota(jnp.int32, (1, 128), 1)
    ins[0].wait()
    outs[0].start()
    for copy in ins[1:]:
        copy.start()
    codes.wait()

    block = heat_v.shape[0] * by * 128

    row_of = lax.broadcasted_iota(jnp.int32, (found.shape[0], 128), 0)

    def fetch(cell, j):
        place = jnp.right_shift(cell, 7)
        row = heat_v[jnp.right_shift(place, by.bit_length() - 1), pl.ds(place & (by - 1), 1), :]
        return pltpu.roll(row, (j - cell) & 127, 1)

    def columns(q, total):
        for k in range(16):
            j = 16 * q + k
            final = code[0, S + j]
            value = fetch(final & (block - 1), j)
            number = jnp.right_shift(final, block.bit_length() - 1)
            total = jnp.where((row_of == number) & (lane == j), value, total)
        return total

    found[...] = lax.fori_loop(0, 8, columns, jnp.zeros(found.shape, F32))

    for copy, after in zip(ins[1:], outs[1:]):
        copy.wait()
        after.start()

    def quad(q, carry):
        counts = [code[0, S + 128 + 4 * q + t] for t in range(4)]

        @pl.when(functools.reduce(jnp.maximum, counts) > 1)
        def _():
            def column(j, carry):
                @pl.when(code[0, S + 128 + j] > 1)
                def _():
                    def one(t, carry):
                        cell = code[0, t * 128 + j]

                        @pl.when(cell >= 0)
                        def _():
                            target = pl.ds(t, 1)
                            found[target, :] = jnp.where(lane == j, fetch(cell, j), found[target, :])

                        return carry

                    lax.fori_loop(0, jnp.right_shift(code[0, S + j], block.bit_length() - 1), one, 0)

                return carry

            lax.fori_loop(4 * q, 4 * q + 4, column, 0)

        return carry

    lax.fori_loop(0, 32, quad, 0)
    for copy in outs:
        copy.wait()


def sum_kernel(
    dims, cost, found_hbm, recorded_hbm, model_out, odds_out, found, recorded, red_a, mid_b, red_b, mid_c, red_c, load_sem,
    rs_sem, rr_sem,
):
    gx, gy, gz = dims
    (ix, iy, iz), plane_device, line_device, _ = places(gx, gy, gz)
    me = iy * gz + iz
    per = S // 128 // gz
    lines = [line_device(k) for k in LINE_ORDER]
    planes = [plane_device(offset) for offset in FAR_FIRST]
    quads = [lax.rem(iz + k, gz) for k in (2, 1, 3)]
    quads = [(other, (ix, iy, other)) for other in quads]
    barrier = pltpu.get_barrier_semaphore()
    partners = lines[:3] + planes + lines[3:]
    for _, device in partners:
        pl.semaphore_signal(barrier, inc=1, device_id=device, device_id_type=MESH)

    def piece(k):
        return pl.ds(pl.multiple_of(k * per, per), per)

    loads = [
        pltpu.make_async_copy(found_hbm, found, load_sem.at[0]),
        pltpu.make_async_copy(recorded_hbm, recorded, load_sem.at[1]),
    ]
    for load in loads:
        load.start()
    loads[0].wait()
    red_a[iz] = found[piece(iz), :]
    pl.semaphore_wait(barrier, len(partners))
    for other, device in quads:
        remote(found.at[piece(other), :], red_a.at[iz], rs_sem.at[0], rr_sem.at[0], device)
    settle(red_a.at[pl.ds(0, gz - 1)], rr_sem.at[0])
    mid_b[...] = jnp.sum(red_a[...], axis=0)
    for other, device in lines:
        remote(mid_b, red_b.at[ix], rs_sem.at[1], rr_sem.at[1], device)
    red_b[ix] = mid_b[...]
    settle(red_b.at[pl.ds(0, gx - 1)], rr_sem.at[1])
    mid_c[...] = jnp.sum(red_b[...], axis=0)
    for _, device in planes:
        remote(mid_c, red_c.at[me], rs_sem.at[2], rr_sem.at[2], device)
    red_c[me] = mid_c[...]
    settle(red_c.at[pl.ds(0, gy * gz - 1)], rr_sem.at[2])
    loads[1].wait()
    values = jnp.sum(red_c[...].reshape(gy, S // 128, 128), axis=0)
    model_out[...] = values
    gap = (values - recorded[...]) / 0.2
    odds_out[0] = cost[0] - 0.5 * (jnp.sum(gap * gap) / S)
    settle(red_a.at[pl.ds(0, gz - 1)], rs_sem.at[0])
    settle(red_b.at[pl.ds(0, gx - 1)], rs_sem.at[1])
    settle(red_c.at[pl.ds(0, gy * gz - 1)], rs_sem.at[2])


def solution(mesh):
    gx, gy, gz = (mesh.shape[name] for name in ("gx", "gy", "gz"))
    nx, ny, nz = MESH_EXTENT_EAST, MESH_EXTENT_NORTH, MESH_EXTENT_UPWARD
    depth, first, second = tables(gx, gy, gz, nx, ny, nz)
    nd = gy * gz
    sub = nz // nd
    part = sub // CHUNKS
    bx, by, bz = nx // gx, ny // gy, nz // gz
    kx_own, ky_own = nx // nd, ny // gx
    per = S // 128 // gz
    smem = pl.BlockSpec(memory_space=pltpu.SMEM)
    hbm = pl.BlockSpec(memory_space=pl.ANY)
    vmem = pl.BlockSpec(memory_space=pltpu.VMEM)
    dma = pltpu.SemaphoreType.DMA
    block = jax.ShapeDtypeStruct((bx, by, bz), F32)

    def body(incumbent, renewed, beta, rho, heat, place, recorded, cost):
        energy, density, kelvin, code = pl.pallas_call(
            functools.partial(kernel, (gx, gy, gz, nx, ny, nz)),
            out_shape=(
                block,
                block,
                block,
                jax.ShapeDtypeStruct((1, S + 256), jnp.int32),
            ),
            in_specs=[smem] + [hbm] * 8,
            out_specs=(hbm, hbm, hbm, vmem),
            scratch_shapes=[
                pltpu.VMEM((3, S), jnp.int32),
                pltpu.VMEM((2, kx_own, ky_own, nz), F32),
                pltpu.VMEM((2, kx_own, ky_own, nz), F32),
                pltpu.VMEM((kx_own * 2 * ky_own, nz), BF16),
                pltpu.VMEM((kx_own * 2 * ky_own, nz), BF16),
                pltpu.VMEM(depth.shape, BF16),
                pltpu.VMEM(first.shape, BF16),
                pltpu.VMEM(second.shape, BF16),
                pltpu.VMEM((CHUNKS, nd * part, kx_own, 128), F32),
                pltpu.VMEM((CHUNKS, nd, part, kx_own, 128), F32),
                pltpu.VMEM((CHUNKS, gx, part, bx, 128), F32),
                pltpu.VMEM((CHUNKS, gx, part, bx, 128), F32),
                pltpu.VMEM((CHUNKS, gy, part * bx // 2, 128), F32),
                pltpu.VMEM((bz * bx // 2, 128), F32),
                pltpu.VMEM((bx, by, bz), F32),
                pltpu.VMEM((bx, by, bz), F32),
                pltpu.VMEM((STEPS, 2, bx + 2, by + 16, bz), F32),
                pltpu.VMEM((bx, by, bz), F32),
                pltpu.VMEM((bx, by, bz), F32),
                pltpu.VMEM((STEPS, 2, GROUPS, 2, SLOTS, bz), F32),
                pltpu.VMEM((STEPS, 2, GROUPS, 2, SLOTS, bz), F32),
                pltpu.VMEM((STEPS, GROUPS, by, bz), F32),
                pltpu.VMEM((STEPS, 2, GROUPS, by, bz), F32),
                dma((8,)),
                dma((3,)),
                dma((CHUNKS,)),
                dma((CHUNKS,)),
                dma((CHUNKS,)),
                dma((CHUNKS,)),
                dma((1,)),
                dma((1,)),
                dma((STEPS, 2)),
                dma((STEPS, 2)),
                dma((STEPS, 2, 2, GROUPS)),
                dma((STEPS, 2, 2, GROUPS)),
            ],
            compiler_params=pltpu.CompilerParams(
                collective_id=0, has_side_effects=True, vmem_limit_bytes=56 * 1024 * 1024
            ),
            cost_estimate=pl.CostEstimate(
                flops=7_000_000_000, bytes_accessed=16_000_000, transcendentals=1_000_000
            ),
        )(
            beta,
            incumbent,
            renewed,
            jnp.asarray(depth),
            jnp.asarray(first),
            jnp.asarray(second),
            rho,
            heat,
            place.T,
        )
        energy, density, kelvin, found = pl.pallas_call(
            functools.partial(read_kernel, by),
            out_shape=(block, block, block, jax.ShapeDtypeStruct((S // 128, 128), F32)),
            in_specs=[hbm] * 4,
            out_specs=(hbm, hbm, hbm, vmem),
            scratch_shapes=[pltpu.SMEM((1, S + 256), jnp.int32)]
            + [pltpu.VMEM((bx, by, bz), F32)] * 3
            + [dma((7,))],
            compiler_params=pltpu.CompilerParams(vmem_limit_bytes=60 * 1024 * 1024),
        )(code, energy, density, kelvin)
        model, odds = pl.pallas_call(
            functools.partial(sum_kernel, (gx, gy, gz)),
            out_shape=(
                jax.ShapeDtypeStruct((S // 128, 128), F32),
                jax.ShapeDtypeStruct((1,), F32),
            ),
            in_specs=[smem, hbm, hbm],
            out_specs=(vmem, smem),
            scratch_shapes=[
                pltpu.VMEM((S // 128, 128), F32),
                pltpu.VMEM((S // 128, 128), F32),
                pltpu.VMEM((gz, per, 128), F32),
                pltpu.VMEM((per, 128), F32),
                pltpu.VMEM((gx, per, 128), F32),
                pltpu.VMEM((per, 128), F32),
                pltpu.VMEM((nd, per, 128), F32),
                dma((2,)),
                dma((3,)),
                dma((3,)),
            ],
            compiler_params=pltpu.CompilerParams(
                collective_id=1, has_side_effects=True, vmem_limit_bytes=60 * 1024 * 1024
            ),
        )(cost, found, recorded.reshape(S // 128, 128))
        return energy, density, kelvin, model.reshape(S), odds

    return jax.shard_map(
        body,
        mesh=mesh,
        in_specs=(
            P(None, ("gy", "gz"), "gx", None),
            P(None, ("gy", "gz"), "gx", None),
            P(),
            P("gx", "gy", "gz"),
            P("gx", "gy", "gz"),
            P(),
            P(),
            P(),
        ),
        out_specs=(P("gx", "gy", "gz"), P("gx", "gy", "gz"), P("gx", "gy", "gz"), P(), P()),
        check_vma=False,
    )
```

```python
import functools
import math

import jax
import jax.numpy as jnp
import ml_dtypes
import numpy as np
from jax import lax
from jax.experimental import pallas as pl
from jax.experimental.pallas import tpu as pltpu
from jax.sharding import PartitionSpec as P

MESH_EXTENT_EAST = 256
MESH_EXTENT_NORTH = 512
MESH_EXTENT_UPWARD = 512
STEPS = 3
S = 4096
CHUNKS = 8
LAG = 3
GROUPS = 4
SLOTS = 8
PIECE = 16
ABL = set()
MESH = pl.DeviceIdType.MESH
F32 = jnp.float32
BF16 = jnp.bfloat16
NT = (((1,), (1,)), ((), ()))


def spectrum(length):
    wave = np.arange(length)
    signed = np.where(wave < length // 2, wave, wave - length).astype(np.float64)
    shape = 1.0 / np.sqrt(1.0 + (signed / 8.0) ** 2)
    return shape / np.sqrt(np.sum(shape * shape))


def waves(places, numbers, length):
    angle = (places[:, None] * numbers[None, :] % length) * (2.0 * math.pi / length)
    scale = spectrum(length)[numbers][None, :]
    return np.cos(angle) * scale, np.sin(angle) * scale


def halves(table):
    high = table.astype(np.float32).astype(ml_dtypes.bfloat16)
    low = (table - high.astype(np.float64)).astype(np.float32).astype(ml_dtypes.bfloat16)
    return high, low


def tables(gx, gy, gz, nx, ny, nz):
    sub = nz // (gy * gz)
    part = sub // CHUNKS
    stacks = []
    for chunk in range(CHUNKS):
        places = np.concatenate(
            [
                z * (nz // gz) + y * sub + chunk * part + np.arange(part)
                for y in range(gy)
                for z in range(gz)
            ]
        )
        cosine, sine = waves(places, np.arange(nz), nz)
        stacks.append(np.concatenate(halves(np.concatenate([cosine, sine]))))
    depth = np.stack(stacks)
    cosine, sine = waves(np.arange(nx), np.arange(nx), nx)
    first = np.concatenate(halves(np.concatenate([cosine, sine])))
    width = ny // gx
    blocks = []
    for block in range(gx):
        cosine, sine = waves(np.arange(ny), block * width + np.arange(width), ny)
        blocks += [cosine.T, -sine.T]
    second = np.stack(halves(np.concatenate(blocks)))
    return depth, first, second


def split(values):
    high = values.astype(BF16)
    return high, (values - high.astype(F32)).astype(BF16)


PLANE_ORDER = [
    (dx, dy, dc)
    for dx, dy in [
        (2, 2), (1, 0), (0, 1), (3, 0), (0, 3), (2, 1), (1, 2), (2, 3),
        (3, 2), (1, 1), (3, 3), (2, 0), (0, 2), (1, 3), (3, 1), (0, 0),
    ]
    for dc in range(2)
    if (dx, dy, dc) != (0, 0, 0)
]
LINE_ORDER = [4, 3, -3, 2, -2, 1, -1]
FAR_FIRST = sorted(PLANE_ORDER, key=lambda o: -min(o[0], 4 - o[0]) - min(o[1], 4 - o[1]))
ROW_ORDER = [(2, 1), (1, 1), (3, 1), (2, 0), (0, 1), (1, 0), (3, 0)]


def places(gx, gy, gz):
    ix, iy, iz = lax.axis_index("gx"), lax.axis_index("gy"), lax.axis_index("gz")
    nx_ring = gy // 2
    x, y_high = lax.rem(iy, nx_ring), iy // nx_ring
    y, core = y_high * (gz // 2) + iz // 2, lax.rem(iz, 2)
    turn = 1 - 2 * core

    def plane(offset):
        dx, dy, dc = offset
        to_x = lax.rem(x + turn * dx + 2 * nx_ring, nx_ring)
        to_y = lax.rem(y + turn * dy + 2 * gz, gz)
        to_core = lax.rem(core + dc, 2)
        to = ((to_y // 2) * nx_ring + to_x, lax.rem(to_y, 2) * 2 + to_core)
        return to[0] * gz + to[1], (ix,) + to

    def line(k):
        other = lax.rem(ix + turn * k + 2 * gx, gx)
        return other, (other, iy, iz)

    def row(offset):
        dx, dy = offset
        other = lax.rem(y_high + dy, 2) * nx_ring + lax.rem(x + turn * dx + 2 * nx_ring, nx_ring)
        return other, (ix, other, iz)

    return (ix, iy, iz), plane, line, row


def greet(plane, line):
    barrier = pltpu.get_barrier_semaphore()
    devices = [line(k)[1] for k in LINE_ORDER[:3]]
    devices += [plane(offset)[1] for offset in FAR_FIRST]
    devices += [line(k)[1] for k in LINE_ORDER[3:]]
    for device in devices:
        pl.semaphore_signal(barrier, inc=1, device_id=device, device_id_type=MESH)


def met():
    pl.semaphore_wait(pltpu.get_barrier_semaphore(), len(PLANE_ORDER) + len(LINE_ORDER))


def remote(src, dst, send_sem, recv_sem, device):
    pltpu.make_async_remote_copy(
        src_ref=src,
        dst_ref=dst,
        send_sem=send_sem,
        recv_sem=recv_sem,
        device_id=device,
        device_id_type=MESH,
    ).start()


def settle(ref, sem):
    pltpu.make_async_copy(ref, ref, sem).wait()


def kernel(
    dims,
    beta,
    inc,
    ren,
    w1_hbm,
    w2_hbm,
    w3_hbm,
    rho0,
    heat0,
    sensors_hbm,
    thr_out,
    rho_out,
    heat_out,
    code_out,
    sensors,
    inc_v,
    ren_v,
    b_high,
    b_low,
    w1,
    w2,
    w3,
    send1,
    got1,
    send2,
    got2,
    send3,
    got3,
    thr,
    inverse,
    state,
    heat_last,
    rho_v,
    hy_send,
    hy_got,
    hz_send,
    hz_got,
    load_sem,
    out_sem,
    s1_sem,
    r1_sem,
    s2_sem,
    r2_sem,
    s3_sem,
    r3_sem,
    hxs_sem,
    hxr_sem,
    hs_sem,
    hr_sem,
):
    gx, gy, gz, nx, ny, nz = dims
    nd = gy * gz
    sub = nz // nd
    part = sub // CHUNKS
    bx, by, bz = nx // gx, ny // gy, nz // gz
    half = bx // 2
    kx_own = nx // nd
    (ix, iy, iz), plane_device, line_device, row_device = places(gx, gy, gz)
    me = iy * gz + iz
    middle = pl.ds(8, by)

    greet(plane_device, line_device)
    loads = [
        pltpu.make_async_copy(inc, inc_v, load_sem.at[0]),
        pltpu.make_async_copy(ren, ren_v, load_sem.at[1]),
        pltpu.make_async_copy(w1_hbm, w1, load_sem.at[2]),
        pltpu.make_async_copy(heat0, state.at[0, 0, pl.ds(1, bx), middle, :], load_sem.at[3]),
        pltpu.make_async_copy(rho0, rho_v, load_sem.at[4]),
        pltpu.make_async_copy(w2_hbm, w2, load_sem.at[5]),
        pltpu.make_async_copy(w3_hbm, w3, load_sem.at[6]),
        pltpu.make_async_copy(sensors_hbm, sensors, load_sem.at[7]),
    ]
    for load in loads:
        load.start()
    lane = lax.broadcasted_iota(jnp.int32, (1, 128), 1)
    sign = jnp.where(lane < 64, -1.0, 1.0).astype(F32)
    first_half = lane < 64

    loads[0].wait()
    loads[1].wait()
    weight = jnp.full((1, 128), beta[0], F32)
    keep = jnp.sqrt(1.0 - weight * weight)[:, :1]
    fresh = weight[:, :1]

    def mix(k, carry):
        for part_of in range(2):
            mixed = keep * inc_v[part_of, k] + fresh * ren_v[part_of, k]
            high, low = split(mixed)
            rows = pl.ds(pl.multiple_of(k * 128 + part_of * 64, 64), 64)
            b_high[rows, :] = high
            b_low[rows, :] = low
        return carry

    lax.fori_loop(0, kx_own, mix, 0)
    loads[2].wait()

    rows1 = nd * part

    def stage1(c):
        flat = send1.at[c].reshape(rows1 * kx_own, 128)
        for q in range(kx_own // 2):
            right = pl.ds(q * 256, 256)
            top = lax.dot_general(w1[c], b_high[right, :], NT, preferred_element_type=F32)
            low = lax.dot_general(
                w1[c, pl.ds(0, 2 * rows1), :], b_low[right, :], NT, preferred_element_type=F32
            )
            total = top[: 2 * rows1] + top[2 * rows1 :] + low
            for side in range(2):
                cut = slice(side * 128, side * 128 + 128)
                cosines = total[:rows1, cut]
                sines = total[rows1:, cut]
                flat[pl.ds(2 * q + side, rows1, stride=kx_own), :] = cosines + sign * pltpu.roll(
                    sines, 64, 1
                )

    def ship1(c):
        for offset in FAR_FIRST:
            other, device = plane_device(offset)
            remote(
                send1.at[c, pl.ds(other * part, part)],
                got1.at[c, me],
                s1_sem.at[c],
                r1_sem.at[c],
                device,
            )
        pltpu.make_async_copy(
            send1.at[c, pl.ds(me * part, part)], got1.at[c, me], r1_sem.at[c]
        ).start()

    def stage2(c):
        settle(got1.at[c], r1_sem.at[c])
        for p in range(part // 2):
            values = jnp.concatenate(
                [got1[c, :, 2 * p + side].reshape(nx, 128) for side in range(2)], axis=1
            )
            high, low = split(values)
            top = jnp.dot(w2[...], high, preferred_element_type=F32)
            bottom = jnp.dot(w2[pl.ds(0, 2 * nx), :], low, preferred_element_type=F32)
            total = top[: 2 * nx] + top[2 * nx :] + bottom
            for side in range(2):
                cut = slice(side * 128, side * 128 + 128)
                result = total[:nx, cut] + sign * pltpu.roll(total[nx:, cut], 64, 1)
                send2[c, :, 2 * p + side] = result.reshape(gx, bx, 128)
        for k in LINE_ORDER:
            other, device = line_device(k)
            remote(send2.at[c, other], got2.at[c, ix], s2_sem.at[c], r2_sem.at[c], device)
        pltpu.make_async_copy(send2.at[c, ix], got2.at[c, ix], r2_sem.at[c]).start()

    def stage3(c):
        settle(got2.at[c], r2_sem.at[c])
        rows = part * bx
        values = jnp.concatenate([got2[c, g].reshape(rows, 128) for g in range(gx)], axis=1)
        high, low = split(values)
        both = jnp.concatenate([high, low], axis=0)
        for t in range(ny // 256):
            columns = pl.ds(t * 256, 256)
            top = jnp.dot(both, w3[0, :, columns], preferred_element_type=F32)
            field = (
                top[:rows]
                + top[rows:]
                + jnp.dot(high, w3[1, :, columns], preferred_element_type=F32)
            )
            energy = 2.0 + 0.6 * jnp.tanh(field)
            for side in range(2):
                tile = energy[:, side * 128 : side * 128 + 128].reshape(part, 2, half, 128)
                near = tile[:, 0].reshape(part * half, 128)
                far = tile[:, 1].reshape(part * half, 128)
                j = 4 * t + 2 * side
                send3[c, j] = jnp.where(first_half, near, pltpu.roll(far, 64, 1))
                send3[c, j + 1] = jnp.where(first_half, pltpu.roll(near, 64, 1), far)
        target = got3.at[
            pl.ds(pl.multiple_of((iy * sub + c * part) * half, part * half), part * half), :
        ]
        for offset in ROW_ORDER:
            other, device = row_device(offset)
            remote(send3.at[c, other], target, s3_sem.at[0], r3_sem.at[0], device)
        pltpu.make_async_copy(send3.at[c, iy], target, r3_sem.at[0]).start()

    def spot(g, slot):
        return lax.rem(g * (SLOTS // 2) + slot // 2 + half - 1, half) + slot % 2 * half

    near_ones = []
    for number, (place, count) in enumerate([(ix, gx), (iy, gy), (iz, gz)]):
        for end in range(2):
            device = [ix, iy, iz]
            device[number] = place + (-1 if end == 0 else 1)
            inner = place > 0 if end == 0 else place < count - 1
            near_ones.append((number, end, inner, tuple(device)))

    outside = jnp.where(lax.rem(lane, 4) < 2, 1.25, 0.0).astype(F32)
    for number, end, inner, device in near_ones:

        @pl.when(jnp.logical_not(inner))
        def _(number=number, end=end):
            for level in range(STEPS):
                if number == 0:
                    x = 0 if end == 0 else bx + 1
                    state[level, 0, x, middle, :] = jnp.full((by, bz), 1.25, F32)
                    state[level, 1, x, middle, :] = jnp.zeros((by, bz), F32)
                elif number == 1:
                    shape = (GROUPS, 1, SLOTS, bz)
                    hy_got[level, end, :, pl.ds(0, 1)] = jnp.full(shape, 1.25, F32)
                    hy_got[level, end, :, pl.ds(1, 1)] = jnp.zeros(shape, F32)
                else:
                    hz_got[level, end] = jnp.broadcast_to(outside, (GROUPS, by, 128))

    def offer(level, g):
        packed = jnp.zeros((by, 128), F32)
        for slot in range(SLOTS):
            x = spot(g, slot) + 1
            heat = state[level, 0, x, middle, :]
            cond = state[level, 1, x, middle, :]
            for f, values in ((0, heat), (1, cond)):
                hy_send[level, 0, g, f, pl.ds(slot, 1), :] = values[:1]
                hy_send[level, 1, g, f, pl.ds(slot, 1), :] = values[by - 1 :]
            ends = jnp.where(lane < 2, pltpu.roll(heat, 1, 1), pltpu.roll(cond, 3, 1))
            if slot:
                ends = pltpu.roll(ends, 4 * slot, 1)
            packed = jnp.where(lane // 4 == slot, ends, packed)
        hz_send[level, g] = packed
        for number, end, inner, device in near_ones:
            if number == 0:
                continue

            @pl.when(inner)
            def _(number=number, end=end, device=device):
                src = hy_send.at[level, end, g] if number == 1 else hz_send.at[level, g]
                dst = (hy_got if number == 1 else hz_got).at[level, 1 - end, g]
                remote(
                    src,
                    dst,
                    hs_sem.at[level, number - 1, end, g],
                    hr_sem.at[level, number - 1, 1 - end, g],
                    device,
                )

    def offer_ends(level):
        for number, end, inner, device in near_ones[:2]:

            @pl.when(inner)
            def _(end=end, device=device):
                remote(
                    state.at[level, :, 1 if end == 0 else bx, middle, :],
                    state.at[level, :, bx + 1 if end == 0 else 0, middle, :],
                    hxs_sem.at[level, end],
                    hxr_sem.at[level, 1 - end],
                    device,
                )

    def accept_ends(level):
        for number, end, inner, device in near_ones[:2]:

            @pl.when(inner)
            def _(end=end):
                settle(
                    state.at[level, :, 0 if end == 0 else bx + 1, middle, :],
                    hxr_sem.at[level, end],
                )

    def accept(level, g):
        for number, end, inner, device in near_ones[2:]:

            @pl.when(inner)
            def _(number=number, end=end):
                settle(
                    (hy_got if number == 1 else hz_got).at[level, end, g],
                    hr_sem.at[level, number - 1, end, g],
                )

        for slot in range(SLOTS):
            x = spot(g, slot) + 1
            for f in range(2):
                row = pl.ds(slot, 1)
                state[level, f, x, pl.ds(7, 1), :] = hy_got[level, 0, g, f, row, :]
                state[level, f, x, pl.ds(8 + by, 1), :] = hy_got[level, 1, g, f, row, :]

    pieces = [pl.ds(k * PIECE, PIECE) for k in range(by // PIECE)]

    def flux_of(level, g, slot, piece):
        x = spot(g, slot) + 1

        def at(f, dx, dy):
            return state[level, f, x + dx, pl.ds(8 + piece.start + dy, PIECE), :]

        heat, cond = at(0, 0, 0), at(1, 0, 0)
        around = [(at(0, dx, dy), at(1, dx, dy)) for dx, dy in ((1, 0), (-1, 0), (0, 1), (0, -1))]
        for end in range(2):
            packed = hz_got[level, end, g, piece, :]
            edge = 0 if end == 0 else 127
            turn = 1 if end == 0 else 127
            pair = []
            for f, values in ((0, heat), (1, cond)):
                shift = (edge - (4 * slot + 2 * f + end)) % 128
                beyond = pltpu.roll(packed, shift, 1) if shift else packed
                pair.append(jnp.where(lane == edge, beyond, pltpu.roll(values, turn, 1)))
            around.append(tuple(pair))
        flux = None
        for heat_side, cond_side in around:
            term = (cond + cond_side) * (heat_side - heat)
            flux = term if flux is None else flux + term
        return x, heat, flux

    def prepare(g, carry):
        accept(0, g)
        for slot in range(SLOTS):
            for piece in pieces:
                x, heat, flux = flux_of(0, g, slot, piece)
                state[1, 0, x, pl.ds(8 + piece.start, PIECE), :] = heat + 0.08 * flux
                inverse[x - 1, piece, :] = -1.0 / heat
        return carry

    def first_step(g, carry):
        for slot in range(0, SLOTS, 2):
            x = spot(g, slot)
            turned = got3[pl.ds(x, bz, stride=half), :].T
            thr[x] = turned[:by]
            thr[half + x] = turned[by:]
        for slot in range(SLOTS):
            x = spot(g, slot)
            rho = rho_v[x]
            growth = jnp.exp(thr[x] * inverse[x]) * (1.0 - rho)
            state[1, 0, x + 1, middle, :] = state[1, 0, x + 1, middle, :] + 0.48 * growth
            rho = rho + 0.64 * growth
            rho_v[x] = rho
            state[1, 1, x + 1, middle, :] = rho * rho

        @pl.when(g == 0)
        def _():
            offer_ends(1)

        offer(1, g)
        return carry

    def grow(level):
        def plane(x, carry):
            rho = rho_v[x]
            growth = jnp.exp(-thr[x] / state[level, 0, x + 1, middle, :]) * (1.0 - rho)
            inverse[x] = 0.48 * growth
            rho = rho + 0.64 * growth
            rho_v[x] = rho
            if level + 1 < STEPS:
                state[level + 1, 1, x + 1, middle, :] = rho * rho
            return carry

        lax.fori_loop(0, bx, plane, 0, unroll=4)

    def later_step(level):
        def group(g, carry):
            @pl.when(g == 0)
            def _():
                accept_ends(level)

            accept(level, g)
            for slot in range(SLOTS):
                for piece in pieces:
                    x, heat, flux = flux_of(level, g, slot, piece)
                    heat = heat + (0.08 * flux + inverse[x - 1, piece, :])
                    if level + 1 < STEPS:
                        state[level + 1, 0, x, pl.ds(8 + piece.start, PIECE), :] = heat
                    else:
                        heat_last[x - 1, piece, :] = heat
            if level + 1 < STEPS:

                @pl.when(g == 0)
                def _():
                    offer_ends(level + 1)

                offer(level + 1, g)

            return carry

        lax.fori_loop(0, GROUPS, group, 0)

    def conduct(x, carry):
        rho = rho_v[x]
        state[0, 1, x + 1, middle, :] = rho * rho
        return carry

    def offer_first(g, carry):
        offer(0, g)
        return carry

    def locate():
        loads[7].wait()
        x = sensors[0:1, :] - ix * bx
        y = sensors[1:2, :] - iy * by
        z = sensors[2:3, :] - iz * bz
        own = (x >= 0) & (x < bx) & (y >= 0) & (y < by) & (z >= 0) & (z < bz)
        code = jnp.where(own, (x * by + y) * bz + z, -1)
        cells = [code[:, t * 128 : t * 128 + 128] for t in range(S // 128)]
        last_one = functools.reduce(
            jnp.maximum, [jnp.where(c >= 0, c + t * (bx * by * bz), -1) for t, c in enumerate(cells)]
        )
        count = functools.reduce(jnp.add, [jnp.where(c >= 0, 1, 0) for c in cells])
        code_out[...] = jnp.concatenate([code, last_one, count], axis=1)

    stage1(0)
    met()

    def pipeline(i, carry):
        @pl.when((i > 0) & (i < CHUNKS))
        def _():
            stage1(i)

        @pl.when(i < CHUNKS)
        def _():
            ship1(i)

        @pl.when(i == 0)
        def _():
            loads[3].wait()
            loads[4].wait()
            lax.fori_loop(0, bx, conduct, 0)
            offer_ends(0)
            lax.fori_loop(0, GROUPS, offer_first, 0)
            loads[5].wait()
            loads[6].wait()

        @pl.when((i >= 1) & (i <= CHUNKS))
        def _():
            stage2(i - 1)

        @pl.when(i == 2)
        def _():
            locate()
            accept_ends(0)

        @pl.when((i >= 2) & (i < 2 + GROUPS))
        def _():
            prepare(i - 2, 0)

        @pl.when(i >= LAG)
        def _():
            stage3(i - LAG)

        return carry

    lax.fori_loop(0, CHUNKS + LAG, pipeline, 0)

    settle(got3, r3_sem.at[0])
    lax.fori_loop(0, GROUPS, first_step, 0)
    thr_copy = pltpu.make_async_copy(thr, thr_out, out_sem.at[0])
    thr_copy.start()
    rho_copy = pltpu.make_async_copy(rho_v, rho_out, out_sem.at[2])
    for level in range(1, STEPS):
        grow(level)
        if level + 1 == STEPS:
            rho_copy.start()
        later_step(level)
    heat_copy = pltpu.make_async_copy(heat_last, heat_out, out_sem.at[1])
    heat_copy.start()

    def drain_chunk(c, carry):
        settle(send1.at[c, pl.ds(0, (nd - 1) * part)], s1_sem.at[c])
        settle(send2.at[c, pl.ds(0, gx - 1)], s2_sem.at[c])
        return carry

    lax.fori_loop(0, CHUNKS, drain_chunk, 0)
    settle(send3.at[:, pl.ds(0, gy - 1)], s3_sem.at[0])
    for number, end, inner, device in near_ones:

        @pl.when(inner)
        def _(number=number, end=end):
            for level in range(STEPS):
                if number == 0:
                    settle(
                        state.at[level, :, 1 if end == 0 else bx, middle, :],
                        hxs_sem.at[level, end],
                    )
                    continue
                for g in range(GROUPS):
                    settle(
                        hy_send.at[level, end, g] if number == 1 else hz_send.at[level, g],
                        hs_sem.at[level, number - 1, end, g],
                    )

    thr_copy.wait()
    heat_copy.wait()
    rho_copy.wait()


def read_kernel(
    by, code_hbm, thr, rho, heat, thr_out, rho_out, heat_out, found, code, thr_v, rho_v, heat_v, sem
):
    codes = pltpu.make_async_copy(code_hbm, code, sem.at[6])
    ins = [
        pltpu.make_async_copy(src, dst, sem.at[k])
        for k, (src, dst) in enumerate(((heat, heat_v), (thr, thr_v), (rho, rho_v)))
    ]
    outs = [
        pltpu.make_async_copy(src, dst, sem.at[3 + k])
        for k, (src, dst) in enumerate(((heat_v, heat_out), (thr_v, thr_out), (rho_v, rho_out)))
    ]
    codes.start()
    ins[0].start()
    lane = lax.broadcasted_iota(jnp.int32, (1, 128), 1)
    ins[0].wait()
    outs[0].start()
    for copy in ins[1:]:
        copy.start()
    codes.wait()

    block = heat_v.shape[0] * by * 128

    row_of = lax.broadcasted_iota(jnp.int32, (found.shape[0], 128), 0)

    def fetch(cell, j):
        place = jnp.right_shift(cell, 7)
        row = heat_v[jnp.right_shift(place, by.bit_length() - 1), pl.ds(place & (by - 1), 1), :]
        return pltpu.roll(row, (j - cell) & 127, 1)

    def columns(q, total):
        for k in range(16):
            j = 16 * q + k
            final = code[0, S + j]
            value = fetch(final & (block - 1), j)
            number = jnp.right_shift(final, block.bit_length() - 1)
            total = jnp.where((row_of == number) & (lane == j), value, total)
        return total

    found[...] = lax.fori_loop(0, 8, columns, jnp.zeros(found.shape, F32))

    for copy, after in zip(ins[1:], outs[1:]):
        copy.wait()
        after.start()

    def quad(q, carry):
        counts = [code[0, S + 128 + 4 * q + t] for t in range(4)]

        @pl.when(functools.reduce(jnp.maximum, counts) > 1)
        def _():
            def column(j, carry):
                @pl.when(code[0, S + 128 + j] > 1)
                def _():
                    def one(t, carry):
                        cell = code[0, t * 128 + j]

                        @pl.when(cell >= 0)
                        def _():
                            target = pl.ds(t, 1)
                            found[target, :] = jnp.where(lane == j, fetch(cell, j), found[target, :])

                        return carry

                    lax.fori_loop(0, jnp.right_shift(code[0, S + j], block.bit_length() - 1), one, 0)

                return carry

            lax.fori_loop(4 * q, 4 * q + 4, column, 0)

        return carry

    lax.fori_loop(0, 32, quad, 0)
    for copy in outs:
        copy.wait()


def sum_kernel(
    dims, cost, found_hbm, recorded_hbm, model_out, odds_out, found, recorded, red_a, mid_b, red_b, mid_c, red_c, load_sem,
    rs_sem, rr_sem,
):
    gx, gy, gz = dims
    (ix, iy, iz), plane_device, line_device, _ = places(gx, gy, gz)
    me = iy * gz + iz
    per = S // 128 // gz
    lines = [line_device(k) for k in LINE_ORDER]
    planes = [plane_device(offset) for offset in FAR_FIRST]
    quads = [lax.rem(iz + k, gz) for k in (2, 1, 3)]
    quads = [(other, (ix, iy, other)) for other in quads]
    barrier = pltpu.get_barrier_semaphore()
    partners = lines[:3] + planes + lines[3:]
    for _, device in partners:
        pl.semaphore_signal(barrier, inc=1, device_id=device, device_id_type=MESH)

    def piece(k):
        return pl.ds(pl.multiple_of(k * per, per), per)

    loads = [
        pltpu.make_async_copy(found_hbm, found, load_sem.at[0]),
        pltpu.make_async_copy(recorded_hbm, recorded, load_sem.at[1]),
    ]
    for load in loads:
        load.start()
    loads[0].wait()
    red_a[iz] = found[piece(iz), :]
    pl.semaphore_wait(barrier, len(partners))
    for other, device in quads:
        remote(found.at[piece(other), :], red_a.at[iz], rs_sem.at[0], rr_sem.at[0], device)
    settle(red_a.at[pl.ds(0, gz - 1)], rr_sem.at[0])
    mid_b[...] = jnp.sum(red_a[...], axis=0)
    for other, device in lines:
        remote(mid_b, red_b.at[ix], rs_sem.at[1], rr_sem.at[1], device)
    red_b[ix] = mid_b[...]
    settle(red_b.at[pl.ds(0, gx - 1)], rr_sem.at[1])
    mid_c[...] = jnp.sum(red_b[...], axis=0)
    for _, device in planes:
        remote(mid_c, red_c.at[me], rs_sem.at[2], rr_sem.at[2], device)
    red_c[me] = mid_c[...]
    settle(red_c.at[pl.ds(0, gy * gz - 1)], rr_sem.at[2])
    loads[1].wait()
    values = jnp.sum(red_c[...].reshape(gy, S // 128, 128), axis=0)
    model_out[...] = values
    gap = (values - recorded[...]) / 0.2
    odds_out[0] = cost[0] - 0.5 * (jnp.sum(gap * gap) / S)
    settle(red_a.at[pl.ds(0, gz - 1)], rs_sem.at[0])
    settle(red_b.at[pl.ds(0, gx - 1)], rs_sem.at[1])
    settle(red_c.at[pl.ds(0, gy * gz - 1)], rs_sem.at[2])


def solution(mesh):
    gx, gy, gz = (mesh.shape[name] for name in ("gx", "gy", "gz"))
    nx, ny, nz = MESH_EXTENT_EAST, MESH_EXTENT_NORTH, MESH_EXTENT_UPWARD
    depth, first, second = tables(gx, gy, gz, nx, ny, nz)
    nd = gy * gz
    sub = nz // nd
    part = sub // CHUNKS
    bx, by, bz = nx // gx, ny // gy, nz // gz
    kx_own, ky_own = nx // nd, ny // gx
    per = S // 128 // gz
    smem = pl.BlockSpec(memory_space=pltpu.SMEM)
    hbm = pl.BlockSpec(memory_space=pl.ANY)
    vmem = pl.BlockSpec(memory_space=pltpu.VMEM)
    dma = pltpu.SemaphoreType.DMA
    block = jax.ShapeDtypeStruct((bx, by, bz), F32)

    def body(incumbent, renewed, beta, rho, heat, place, recorded, cost):
        energy, density, kelvin, code = pl.pallas_call(
            functools.partial(kernel, (gx, gy, gz, nx, ny, nz)),
            out_shape=(
                block,
                block,
                block,
                jax.ShapeDtypeStruct((1, S + 256), jnp.int32),
            ),
            in_specs=[smem] + [hbm] * 8,
            out_specs=(hbm, hbm, hbm, vmem),
            scratch_shapes=[
                pltpu.VMEM((3, S), jnp.int32),
                pltpu.VMEM((2, kx_own, ky_own, nz), F32),
                pltpu.VMEM((2, kx_own, ky_own, nz), F32),
                pltpu.VMEM((kx_own * 2 * ky_own, nz), BF16),
                pltpu.VMEM((kx_own * 2 * ky_own, nz), BF16),
                pltpu.VMEM(depth.shape, BF16),
                pltpu.VMEM(first.shape, BF16),
                pltpu.VMEM(second.shape, BF16),
                pltpu.VMEM((CHUNKS, nd * part, kx_own, 128), F32),
                pltpu.VMEM((CHUNKS, nd, part, kx_own, 128), F32),
                pltpu.VMEM((CHUNKS, gx, part, bx, 128), F32),
                pltpu.VMEM((CHUNKS, gx, part, bx, 128), F32),
                pltpu.VMEM((CHUNKS, gy, part * bx // 2, 128), F32),
                pltpu.VMEM((bz * bx // 2, 128), F32),
                pltpu.VMEM((bx, by, bz), F32),
                pltpu.VMEM((bx, by, bz), F32),
                pltpu.VMEM((STEPS, 2, bx + 2, by + 16, bz), F32),
                pltpu.VMEM((bx, by, bz), F32),
                pltpu.VMEM((bx, by, bz), F32),
                pltpu.VMEM((STEPS, 2, GROUPS, 2, SLOTS, bz), F32),
                pltpu.VMEM((STEPS, 2, GROUPS, 2, SLOTS, bz), F32),
                pltpu.VMEM((STEPS, GROUPS, by, bz), F32),
                pltpu.VMEM((STEPS, 2, GROUPS, by, bz), F32),
                dma((8,)),
                dma((3,)),
                dma((CHUNKS,)),
                dma((CHUNKS,)),
                dma((CHUNKS,)),
                dma((CHUNKS,)),
                dma((1,)),
                dma((1,)),
                dma((STEPS, 2)),
                dma((STEPS, 2)),
                dma((STEPS, 2, 2, GROUPS)),
                dma((STEPS, 2, 2, GROUPS)),
            ],
            compiler_params=pltpu.CompilerParams(
                collective_id=0, has_side_effects=True, vmem_limit_bytes=56 * 1024 * 1024
            ),
            cost_estimate=pl.CostEstimate(
                flops=7_000_000_000, bytes_accessed=16_000_000, transcendentals=1_000_000
            ),
        )(
            beta,
            incumbent,
            renewed,
            jnp.asarray(depth),
            jnp.asarray(first),
            jnp.asarray(second),
            rho,
            heat,
            place.T,
        )
        energy, density, kelvin, found = pl.pallas_call(
            functools.partial(read_kernel, by),
            out_shape=(block, block, block, jax.ShapeDtypeStruct((S // 128, 128), F32)),
            in_specs=[hbm] * 4,
            out_specs=(hbm, hbm, hbm, vmem),
            scratch_shapes=[pltpu.SMEM((1, S + 256), jnp.int32)]
            + [pltpu.VMEM((bx, by, bz), F32)] * 3
            + [dma((7,))],
            compiler_params=pltpu.CompilerParams(vmem_limit_bytes=60 * 1024 * 1024),
        )(code, energy, density, kelvin)
        model, odds = pl.pallas_call(
            functools.partial(sum_kernel, (gx, gy, gz)),
            out_shape=(
                jax.ShapeDtypeStruct((S // 128, 128), F32),
                jax.ShapeDtypeStruct((1,), F32),
            ),
            in_specs=[smem, hbm, hbm],
            out_specs=(vmem, smem),
            scratch_shapes=[
                pltpu.VMEM((S // 128, 128), F32),
                pltpu.VMEM((S // 128, 128), F32),
                pltpu.VMEM((gz, per, 128), F32),
                pltpu.VMEM((per, 128), F32),
                pltpu.VMEM((gx, per, 128), F32),
                pltpu.VMEM((per, 128), F32),
                pltpu.VMEM((nd, per, 128), F32),
                dma((2,)),
                dma((3,)),
                dma((3,)),
            ],
            compiler_params=pltpu.CompilerParams(
                collective_id=1, has_side_effects=True, vmem_limit_bytes=60 * 1024 * 1024
            ),
        )(cost, found, recorded.reshape(S // 128, 128))
        return energy, density, kelvin, model.reshape(S), odds

    return jax.shard_map(
        body,
        mesh=mesh,
        in_specs=(
            P(None, ("gy", "gz"), "gx", None),
            P(None, ("gy", "gz"), "gx", None),
            P(),
            P("gx", "gy", "gz"),
            P("gx", "gy", "gz"),
            P(),
            P(),
            P(),
        ),
        out_specs=(P("gx", "gy", "gz"), P("gx", "gy", "gz"), P("gx", "gy", "gz"), P(), P()),
        check_vma=False,
    )
```
